256 devices in a mesh: row: 32 (over y, z), col: 8 (over x, core).
Axes of the slice: x: 4, y: 4, z: 8, core: 2. Of those that a mesh axis runs over, the one named last changes fastest.
Arguments:
- rhs: float32 [32, 524288], P(None, ('row', 'col')), may hold values from -5 to 7
- coords: float32 [3, 524288], P(None, ('row', 'col')), may hold values from 0 to 16, as said below
- nugget: float32 [524288], P(('row', 'col')), may hold values from 1.5 to 3
- near_ids: int32 [1024, 3], P(('row', 'col')), may hold values from -1 to 1023, as said below
- basis: float32 [10, 128, 524288], P(None, None, ('row', 'col')), may hold values from -6 to 6
Outputs:
- solution: float32 [32, 524288], P(None, ('row', 'col'))
- residual: float32 [32, 524288], P(None, ('row', 'col'))
The draws below stay inside these ranges and needn't reach their ends.
Inputs may be any that keep to these rules, and one draw needn't show every extreme that they name: `near_ids`: row i lists leaf i and some of the leaves i - 1 to i + 1 inside the range, each at most once, in any order; the other slots hold -1; the first and last leaf of each device's block of 4 list all such leaves inside the range. `coords`: each leaf's points lie in a unit box with an integer corner; consecutive leaves lie in boxes that share a face.
All inputs are finite; a program needn't handle non-finite values.
Results may differ from the reference program's by a relative error of at most 0.0003.
Values sent between devices are 32-bit elements; how exact they have to be, the bound alone decides.
A program may use at most 128 MiB of HBM per device.

```python
import jax
import jax.numpy as jnp
from jax import lax

LEAF = 512
RANK = 128
NRHS = 32
ITERS = 4
REACH = 1
LEAF_DEV = 4
WIN = 3
NLEAF = 1024
NPTS = 524288
LEAF_BITS = 2
DEV_BITS = 8
LEVELS = 10


def snake_corner(leaf):
    total_bits = DEV_BITS + LEAF_BITS
    side = 2 ** (total_bits // 3)
    first = leaf % side
    line = leaf // side
    second_raw = line % side
    plane = line // side
    first = jnp.where(line % 2 == 0, first, side - 1 - first)
    second = jnp.where(plane % 2 == 0, second_raw, side - 1 - second_raw)
    return jnp.stack([first, second, plane])


def draw_coords(key, part):
    key = jax.random.fold_in(key, 11)
    leaf = jnp.arange(NPTS, dtype=jnp.int32) // LEAF
    corner = snake_corner(leaf).astype(jnp.float32)
    jitter = jax.random.uniform(key, (3, NPTS), jnp.float32)
    return corner + jitter


def draw_rhs(key, part):
    key = jax.random.fold_in(key, 23)
    rough_key, mean_key = jax.random.split(key)
    rough = jnp.clip(jax.random.normal(rough_key, (NRHS, NPTS), jnp.float32), -5.0, 5.0)
    offset = jax.random.uniform(mean_key, (NRHS, NLEAF, 1), jnp.float32, 0.0, 1.5)
    return (rough.reshape(NRHS, NLEAF, LEAF) + offset).reshape(NRHS, NPTS)


def draw_near_ids(key, part):
    key = jax.random.fold_in(key, 37)
    rate_key, roll_key, order_key = jax.random.split(key, 3)
    leaf = jnp.arange(NLEAF, dtype=jnp.int32)[:, None]
    offsets = jnp.arange(WIN, dtype=jnp.int32)[None, :] - REACH
    target = leaf + offsets
    inside = (target >= 0) & (target < NLEAF)
    rates = jnp.repeat(jax.random.randint(rate_key, (NLEAF // 8,), 10, 100), 8)[:, None]
    rolls = jax.random.randint(roll_key, (NLEAF, WIN), 0, 100)
    edge = (leaf % LEAF_DEV == 0) | (leaf % LEAF_DEV == LEAF_DEV - 1)
    keep = inside & ((rolls < rates) | (offsets == 0) | edge)
    listed = jnp.where(keep, target, -1)
    scores = jax.random.randint(order_key, (NLEAF, WIN), 0, 2 ** 20) * WIN + jnp.arange(WIN, dtype=jnp.int32)[None, :]
    order = jnp.argsort(scores, axis=1)
    return jnp.take_along_axis(listed, order, axis=1).astype(jnp.int32)


def block_levels(own_key, dims, cuts, low, high):
    loudness = 1.0
    for dim, shards_of in cuts:
        draws = jax.random.uniform(jax.random.fold_in(jax.random.fold_in(own_key, 6), dim), (shards_of,), jnp.float32, low / len(cuts), high / len(cuts))
        loudness = loudness * jnp.repeat(jnp.exp(draws), dims[dim] // shards_of).reshape((-1,) + (1,) * (len(dims) - 1 - dim))
    return loudness


def scatter_about(rng, extent, scale, limit, cuts=(), kind=jnp.bfloat16):
    values = jax.random.normal(rng, extent, jnp.float32) * scale
    if len(cuts) > 0:
        values = block_levels(rng, extent, cuts, -0.22, 0.18) * values
    return jnp.clip(values, min=-limit, max=limit).astype(kind)


def setup_inputs(seed: int = 0) -> dict:
    arg_keys = jax.random.split(jax.random.key(seed), 6)
    rhs = draw_rhs(jax.random.fold_in(arg_keys[5], 71), 0)
    coords = draw_coords(jax.random.fold_in(arg_keys[5], 71), 0)
    nugget = jnp.clip(1.5 + 1.5 * jax.random.uniform(arg_keys[2], (NPTS,), jnp.float32) ** block_levels(arg_keys[2], (NPTS,), ((0, 256),), -0.2, 0.2), 1.5, 3.0)
    near_ids = draw_near_ids(jax.random.fold_in(arg_keys[5], 71), 0)
    basis = scatter_about(arg_keys[4], (LEVELS, RANK, NPTS), 1.0, 6.0, ((2, 256),), jnp.float32)
    return {"rhs": rhs, "coords": coords, "nugget": nugget, "near_ids": near_ids, "basis": basis}


root_three = 1.7320508075688772
spacing_factor = 1.6

def matern(square_dist):
    length = spacing_factor * LEAF ** (-1.0 / 3.0)
    scaled = root_three * jnp.sqrt(square_dist) / length
    return (1.0 + scaled) * jnp.exp(-scaled)

def window_mask(near_ids, first_leaf, count):
    leaves = first_leaf + jnp.arange(count, dtype=jnp.int32)
    offsets = jnp.arange(WIN, dtype=jnp.int32) - REACH
    target = leaves[None, :] + offsets[:, None]
    matches = near_ids.T[None, :, :] == target[:, None, :]
    return jnp.any(matches, axis=1).astype(jnp.float32)

def tile_block(own_coords, far_coords, weight):
    spread = own_coords[:, :, :, None] - far_coords[:, :, None, :]
    square_dist = lax.optimization_barrier(jnp.sum(spread * spread, axis=0))
    return matern(square_dist) * (weight / (16 * WIN))[:, None, None]

def near_field(field, coords, mask):
    margin = REACH * LEAF
    blocks = NLEAF // LEAF_DEV
    field_pad = jnp.pad(field, ((0, 0), (margin, margin)))
    coord_pad = jnp.pad(coords, ((0, 0), (margin, margin)))
    own = coords.reshape(3, blocks, LEAF_DEV, LEAF).transpose(1, 0, 2, 3)
    total = jnp.zeros((NRHS, NPTS), jnp.float32)
    for offset in range(WIN):
        far = coord_pad[:, offset * LEAF:offset * LEAF + NPTS].reshape(3, blocks, LEAF_DEV, LEAF).transpose(1, 0, 2, 3)
        segment = field_pad[:, offset * LEAF:offset * LEAF + NPTS].reshape(NRHS, blocks, LEAF_DEV, LEAF).transpose(1, 0, 2, 3)
        weight = mask[offset].reshape(blocks, LEAF_DEV)

        def one_block(inputs):
            own_block, far_block, seg_block, wgt_block = inputs
            tile_set = tile_block(own_block, far_block, wgt_block)
            return jnp.einsum('bij,rbj->rbi', tile_set, seg_block, precision=lax.Precision.HIGHEST)
        part_sum = lax.map(one_block, (own, far, segment, weight))
        total = total + part_sum.transpose(1, 0, 2, 3).reshape(NRHS, NPTS)
    return total

def far_field(field, basis):
    total = jnp.zeros((NRHS, NPTS), jnp.float32)
    for level in range(LEVELS):
        cluster = LEAF * 2 ** (level + 1)
        grouped = basis[level].reshape(RANK, NPTS // cluster, cluster)
        values = field.reshape(NRHS, NPTS // cluster, cluster)
        skeleton = jnp.einsum('kcs,rcs->crk', grouped, values, precision=lax.Precision.HIGHEST)
        spread_back = jnp.einsum('kcs,crk->rcs', grouped, skeleton, precision=lax.Precision.HIGHEST)
        total = total + spread_back.reshape(NRHS, NPTS) / cluster
    return total

def reference(rhs, coords, nugget, near_ids, basis):
    mask = window_mask(near_ids, jnp.int32(0), NLEAF)

    def operate(field):
        return nugget[None, :] * field + near_field(field, coords, mask) + far_field(field, basis)
    solution = jnp.zeros((NRHS, NPTS), jnp.float32)
    residual = rhs
    direction = rhs
    norm_now = lax.optimization_barrier(jnp.sum(residual * residual, axis=1))
    for step in range(ITERS):
        image = operate(direction)
        step_size = norm_now / lax.optimization_barrier(jnp.sum(direction * image, axis=1))
        solution = solution + step_size[:, None] * direction
        residual = residual - step_size[:, None] * image
        norm_next = lax.optimization_barrier(jnp.sum(residual * residual, axis=1))
        direction = residual + (norm_next / norm_now)[:, None] * direction
        norm_now = norm_next
    return (solution, residual)
```

```python
import functools

import jax
import jax.numpy as jnp
from jax import lax
from jax.experimental import pallas as pl
from jax.experimental.pallas import tpu as pltpu
from jax.sharding import PartitionSpec as P

LEAF = 512
ITERS = 4
RANK = 128
NRHS = 32
LEVELS = 10
LEAVES = 4
WIDTH = LEAF * LEAVES
NC, NZ, NY = 8, 8, 4
NDEV = NC * NZ * NY
MESH = pl.DeviceIdType.MESH
F32 = jnp.float32
BF16 = jnp.bfloat16

ROOT_THREE = 1.7320508075688772
LENGTH = 1.6 * LEAF ** (-1.0 / 3.0)
LOG2E = 1.4426950408889634
STRIP = 32


def dot_nn(a, b):
    return lax.dot_general(a, b, (((1,), (0,)), ((), ())), preferred_element_type=F32)


def dot_nt(a, b):
    return lax.dot_general(a, b, (((1,), (1,)), ((), ())), preferred_element_type=F32)


def split3(value):
    first = value.astype(BF16)
    rest = value - first.astype(F32)
    second = rest.astype(BF16)
    third = (rest - second.astype(F32)).astype(BF16)
    return jnp.concatenate([first, second, third], axis=0)


def product(dot, pieces, high, low):
    rows = pieces.shape[0] // 3
    big = dot(pieces, high)
    small = dot(pieces[: 2 * rows], low)
    return (big[:rows] + (big[rows : 2 * rows] + small[:rows])) + (big[2 * rows :] + small[rows:])


def kernel(
    rhs_ref,
    coords_ref,
    nugget_ref,
    ids_ref,
    basis_ref,
    sol_ref,
    res_ref,
    stage,
    bh,
    bl,
    eh,
    el,
    ccol,
    chalo,
    fs,
    fh,
    dirn,
    wvec,
    qvec,
    zvec,
    halo,
    prs,
    p01,
    recv1,
    recv01,
    zsend,
    recv2,
    recv20,
    ysend,
    recv3,
    tfull,
    scs,
    scr,
    bsem,
    csem,
    hsem,
    s1,
    s01,
    s2,
    s20,
    s3,
    sg1,
    sg2,
    ssc,
    cs_send,
    hs_send,
    s1_send,
    s01_send,
    s2_send,
    s20_send,
    s3_send,
    sg1_send,
    sg2_send,
    ssc_send,
):
    row = lax.axis_index("row")
    col = lax.axis_index("col")
    yy = row // NZ
    zz = row % NZ
    hh = col // 4
    gg = col % 4
    dev = row * NC + col
    right_dev = (dev + 1) % NDEV
    left_dev = (dev + NDEV - 1) % NDEV
    right = (right_dev // NC, right_dev % NC)
    left = (left_dev // NC, left_dev % NC)
    cpeers = [(row, (col + k) % NC) for k in range(1, NC)]
    zpeers = [(yy * NZ + (zz + k) % NZ, col) for k in range(1, NZ)]
    ypeers = [(((yy + k) % NY) * NZ + zz, col) for k in range(1, NY)]
    quad = [(row, (col // 4) * 4 + (col % 4 + k) % 4) for k in range(1, 4)]
    core = (row, col + 1 - 2 * (col % 2))
    ztwin = (yy * NZ + zz + 1 - 2 * (zz % 2), col)
    my_rows = pl.ds(pl.multiple_of(gg * 8, 8), 8)

    order = list(range(2, LEVELS)) + [0, 1]
    for level in order:
        pltpu.make_async_copy(basis_ref.at[level], stage.at[level], bsem.at[level]).start()
    barrier = pltpu.get_barrier_semaphore()
    greeted = cpeers + zpeers + ypeers + [left, right]
    for peer in greeted:
        pl.semaphore_signal(barrier, inc=1, device_id=peer, device_id_type=MESH)

    def send(src, dst, send_sem, recv_sem, peer):
        pltpu.make_async_remote_copy(
            src_ref=src, dst_ref=dst, send_sem=send_sem, recv_sem=recv_sem, device_id=peer, device_id_type=MESH
        ).start()

    def await_bytes(ref, sem):
        pltpu.make_async_copy(ref, ref, sem).wait()

    lane = lax.broadcasted_iota(jnp.int32, (NRHS, 128), 1)
    sub = lax.broadcasted_iota(jnp.int32, (NRHS, 128), 0)
    hit = (lane % NRHS) == sub

    def as_row(columns):
        spread = jnp.zeros((NRHS, 128), F32)
        for index, column in enumerate(columns):
            spread = jnp.where(hit & (lane // NRHS == index), column, spread)
        return jnp.sum(spread, axis=0, keepdims=True)

    def as_columns(line):
        wide = jnp.where(hit, jnp.broadcast_to(line, (NRHS, 128)), 0.0)
        return [
            jnp.sum(jnp.where(lane // NRHS == index, wide, 0.0), axis=1, keepdims=True)
            for index in range(4)
        ]

    def dots_row():
        r, d, q = res_ref[...], dirn[...], qvec[...]
        return as_row(
            [
                jnp.sum(r * r, axis=1, keepdims=True),
                jnp.sum(d * q, axis=1, keepdims=True),
                jnp.sum(r * q, axis=1, keepdims=True),
                jnp.sum(q * q, axis=1, keepdims=True),
            ]
        )

    def scalar_send(a, phase, peers, base):
        for k, peer in enumerate(peers):
            send(scs.at[a, phase], scr.at[a, base + k], ssc_send.at[a, phase], ssc.at[a, phase], peer)

    def scalar_gather(a, phase, count, base):
        await_bytes(scr.at[a, pl.ds(base, count)], ssc.at[a, phase])
        total = scs[a, phase]
        for k in range(count):
            total = total + scr[a, base + k]
        return total

    def split_level(level):
        value = stage[level]
        rows = slice(level * RANK, (level + 1) * RANK)
        high = value.astype(BF16)
        bh[rows, :] = high
        bl[rows, :] = (value - high.astype(F32)).astype(BF16)

    def load_levels(levels):
        for level in levels:
            pltpu.make_async_copy(basis_ref.at[level], stage.at[level], bsem.at[level]).wait()
            split_level(level)

    def skeleton_pair(a, level):
        rows = slice(level * RANK, (level + 2) * RANK)
        both = product(dot_nt, fs[...], bh[rows, :], bl[rows, :])
        for side in range(2):
            part = both[:, side * RANK : (side + 1) * RANK]
            if level == 2:
                p01[a, side] = part
            else:
                prs[a, side, (level - 4) // 2] = part

    def spread(levels, total):
        scaled = jnp.concatenate([t * (1.0 / (LEAF * 2 ** (level + 1))) for level, t in zip(levels, total)], axis=1)
        pieces = split3(scaled)
        rows = slice(levels[0] * RANK, (levels[-1] + 1) * RANK)
        for start in range(0, WIDTH, 512):
            span = slice(start, start + 512)
            zvec[:, span] += product(dot_nn, pieces, bh[rows, span], bl[rows, span])

    def local_levels():
        for level, cluster in ((0, 2 * LEAF), (1, 4 * LEAF)):
            rows = slice(level * RANK, (level + 1) * RANK)
            for start in range(0, WIDTH, cluster):
                span = slice(start, start + cluster)
                skeleton = product(dot_nt, fs[:, span], bh[rows, span], bl[rows, span])
                pieces = split3(skeleton * (1.0 / cluster))
                zvec[:, span] += product(dot_nn, pieces, bh[rows, span], bl[rows, span])

    def mask_value(leaf, offset):
        target = dev * LEAVES + leaf + offset - 1
        found = (ids_ref[leaf, 0] == target) | (ids_ref[leaf, 1] == target) | (ids_ref[leaf, 2] == target)
        return jnp.where(found & (target >= 0), 1.0, 0.0).astype(F32)

    def near_term(leaf, offset, pieces, block, dot):
        span = slice(leaf * LEAF, (leaf + 1) * LEAF)
        zvec[:, span] += mask_value(leaf, offset) * product(dot, pieces, eh[block], el[block])

    def own_pieces(leaf):
        return fs[:, leaf * LEAF : (leaf + 1) * LEAF]

    def near_diag(leaf):
        near_term(leaf, 1, own_pieces(leaf), leaf, dot_nn)

    def near_pair(leaf):
        near_term(leaf + 1, 0, own_pieces(leaf), 5 + leaf, dot_nn)
        near_term(leaf, 2, own_pieces(leaf + 1), 5 + leaf, dot_nt)

    def near_halo(a):
        for side, leaf, offset, block in ((0, 0, 0, 4), (1, LEAVES - 1, 2, 8)):
            await_bytes(halo.at[a, side], hsem.at[a, side])
            fh[side] = split3(halo[a, side])
            near_term(leaf, offset, fh[side], block, dot_nt)

    def build(block, first_leaf, other):
        def strip(index, carry):
            start = pl.multiple_of(index * STRIP, STRIP)
            here = ccol[pl.ds(first_leaf * LEAF + start, STRIP), :]
            square = None
            for axis in range(3):
                gap = here[:, axis : axis + 1] - other(axis)
                square = gap * gap if square is None else square + gap * gap
            dist = square * lax.rsqrt(jnp.maximum(square, 1e-30))
            factor = ROOT_THREE / LENGTH
            value = (1.0 / 48.0 + (factor / 48.0) * dist) * jnp.exp2(dist * (-factor * LOG2E))
            high = value.astype(BF16)
            eh[block, pl.ds(start, STRIP), :] = high
            el[block, pl.ds(start, STRIP), :] = (value - high.astype(F32)).astype(BF16)
            return carry

        lax.fori_loop(0, LEAF // STRIP, strip, 0)

    def own_row(leaf):
        return lambda axis: coords_ref[axis : axis + 1, leaf * LEAF : (leaf + 1) * LEAF]

    def halo_row(side):
        return lambda axis: chalo[side, axis : axis + 1, :]

    def apply(a, first):
        fs[...] = split3(qvec[...])
        if first:
            for level in range(2, LEVELS, 2):
                load_levels([level, level + 1])
                skeleton_pair(a, level)
            pl.semaphore_wait(barrier, len(greeted))
        else:
            for level in range(2, LEVELS, 2):
                skeleton_pair(a, level)
        for k in range(1, NC):
            other = (col + k) % NC
            rows = pl.ds(pl.multiple_of((other % 4) * 8, 8), 8)
            send(prs.at[a, other // 4, :, rows, :], recv1.at[a, k - 1], s1_send.at[a], s1.at[a], cpeers[k - 1])
        if not first:
            scs[a, 0] = dots_row()
            scalar_send(a, 0, cpeers, 0)
        send(qvec.at[:, 0:LEAF], halo.at[a, 1], hs_send.at[a, 1], hsem.at[a, 1], left)
        send(qvec.at[:, WIDTH - LEAF : WIDTH], halo.at[a, 0], hs_send.at[a, 0], hsem.at[a, 0], right)
        send(p01.at[a, 0], recv01.at[a, 0], s01_send.at[a], s01.at[a], core)
        for k in range(3):
            send(p01.at[a, 1], recv01.at[a, k + 1], s01_send.at[a], s01.at[a], quad[k])
        if first:
            send(coords_ref.at[:, 0:LEAF], chalo.at[1], cs_send.at[1], csem.at[1], left)
            send(coords_ref.at[:, WIDTH - LEAF : WIDTH], chalo.at[0], cs_send.at[0], csem.at[0], right)

        zvec[...] = nugget_ref[...] * qvec[...]
        if first:
            ccol[...] = jnp.transpose(jnp.concatenate([coords_ref[...], jnp.zeros((5, WIDTH), F32)], axis=0))
            for leaf in range(LEAVES):
                build(leaf, leaf, own_row(leaf))
        for leaf in range(LEAVES):
            near_diag(leaf)

        await_bytes(recv1.at[a], s1.at[a])
        for t in range(3):
            total = prs[a, hh, t, my_rows, :]
            for k in range(NC - 1):
                total = total + recv1[a, k, t]
            zsend[a, t] = total
        for k in range(1, NZ):
            send(zsend.at[a, pl.ds(1, 2)], recv2.at[a, k - 1], s2_send.at[a], s2.at[a], zpeers[k - 1])
        send(zsend.at[a, 0], recv20.at[a], s20_send.at[a], s20.at[a], ztwin)
        if not first:
            scs[a, 1] = scalar_gather(a, 0, NC - 1, 0)
            scalar_send(a, 1, zpeers, NC - 1)

        if first:
            for leaf in range(LEAVES - 1):
                build(5 + leaf, leaf, own_row(leaf + 1))
        for leaf in range(LEAVES - 1):
            near_pair(leaf)

        await_bytes(recv2.at[a], s2.at[a])
        await_bytes(recv20.at[a], s20.at[a])
        one = zsend[a, 1]
        two = zsend[a, 2]
        for k in range(1, NZ):
            source = (zz + NZ - k) % NZ
            near_z = jnp.where((hh == 1) | (source // 4 == zz // 4), 1.0, 0.0).astype(F32)
            one = one + near_z * recv2[a, k - 1, 0]
            two = two + recv2[a, k - 1, 1]
        ysend[a] = two
        for k in range(1, NY):
            send(ysend.at[a], recv3.at[a, k - 1], s3_send.at[a], s3.at[a], ypeers[k - 1])
        tfull[a, hh, 0, my_rows, :] = zsend[a, 0] + hh.astype(F32) * recv20[a]
        tfull[a, hh, 1, my_rows, :] = one
        mine = tfull.at[a, hh, pl.ds(0, 2), my_rows, :]
        for k in range(1, NC):
            send(mine, mine, sg1_send.at[a], sg1.at[a], cpeers[k - 1])
        if not first:
            scs[a, 2] = scalar_gather(a, 1, NZ - 1, NC - 1)
            scalar_send(a, 2, ypeers, NC + NZ - 2)

        if first:
            load_levels([0, 1])
            for side, leaf, block in ((0, 0, 4), (1, LEAVES - 1, 8)):
                await_bytes(chalo.at[side], csem.at[side])
                build(block, leaf, halo_row(side))
        local_levels()

        await_bytes(recv3.at[a], s3.at[a])
        top = ysend[a]
        for k in range(1, NY):
            source = (yy + NY - k) % NY
            near_y = jnp.where((hh == 1) | (source // 2 == yy // 2), 1.0, 0.0).astype(F32)
            top = top + near_y * recv3[a, k - 1]
        tfull[a, hh, 2, my_rows, :] = top
        mine = tfull.at[a, hh, 2, my_rows, :]
        for k in range(1, NC):
            send(mine, mine, sg2_send.at[a], sg2.at[a], cpeers[k - 1])

        near_halo(a)
        await_bytes(recv01.at[a], s01.at[a])
        await_bytes(recv1.at[a, :, pl.ds(0, 2)], sg1.at[a])
        lower = [
            p01[a, 0] + recv01[a, 0],
            (p01[a, 1] + recv01[a, 1]) + (recv01[a, 2] + recv01[a, 3]),
            tfull[a, 0, 0],
            tfull[a, 1, 0],
            tfull[a, 0, 1],
            tfull[a, 1, 1],
        ]
        spread(list(range(2, 8)), lower)
        await_bytes(recv1.at[a, :, 0], sg2.at[a])
        spread([8, 9], [tfull[a, 0, 2], tfull[a, 1, 2]])

    def steps(total):
        norm, curve, cross, square = as_columns(total)
        step = norm / curve
        fresh = jnp.maximum(norm - 2.0 * step * cross + step * step * square, 0.0)
        return step, fresh / norm

    start = rhs_ref[...]
    sol_ref[...] = jnp.zeros_like(sol_ref)
    res_ref[...] = start
    dirn[...] = start
    qvec[...] = start
    apply(0, True)
    image = zvec[...]
    await_bytes(halo.at[0, 0], hs_send.at[0, 0])
    await_bytes(halo.at[0, 1], hs_send.at[0, 1])
    wvec[...] = image
    qvec[...] = image

    def iteration(a, carry):
        apply(a, False)
        total = scalar_gather(a, 2, NY - 1, NC + NZ - 2)
        step, ratio = steps(total)
        await_bytes(halo.at[a, 0], hs_send.at[a, 0])
        await_bytes(halo.at[a, 1], hs_send.at[a, 1])
        q = qvec[...]
        d = dirn[...]
        sol_ref[...] += step * d
        r = res_ref[...] - step * q
        res_ref[...] = r
        dirn[...] = r + ratio * d
        w = wvec[...] - step * zvec[...]
        wvec[...] = w
        qvec[...] = w + ratio * q
        return carry

    lax.fori_loop(1, ITERS, iteration, 0)

    last = ITERS
    scs[last, 0] = dots_row()
    scalar_send(last, 0, cpeers, 0)
    scs[last, 1] = scalar_gather(last, 0, NC - 1, 0)
    scalar_send(last, 1, zpeers, NC - 1)
    scs[last, 2] = scalar_gather(last, 1, NZ - 1, NC - 1)
    scalar_send(last, 2, ypeers, NC + NZ - 2)
    step, _ = steps(scalar_gather(last, 2, NY - 1, NC + NZ - 2))
    sol_ref[...] += step * dirn[...]
    res_ref[...] += -step * qvec[...]

    def drain(a, carry):
        await_bytes(recv1.at[a], s1_send.at[a])
        await_bytes(recv01.at[a], s01_send.at[a])
        await_bytes(recv2.at[a], s2_send.at[a])
        await_bytes(recv20.at[a], s20_send.at[a])
        await_bytes(recv3.at[a], s3_send.at[a])
        await_bytes(recv1.at[a, :, pl.ds(0, 2)], sg1_send.at[a])
        await_bytes(recv1.at[a, :, 0], sg2_send.at[a])
        return carry

    def drain_scalars(a, carry):
        for phase, (base, count) in enumerate(((0, NC - 1), (NC - 1, NZ - 1), (NC + NZ - 2, NY - 1))):
            await_bytes(scr.at[a, pl.ds(base, count)], ssc_send.at[a, phase])
        return carry

    lax.fori_loop(0, ITERS, drain, 0)
    lax.fori_loop(1, ITERS + 1, drain_scalars, 0)
    for side in range(2):
        await_bytes(chalo.at[side], cs_send.at[side])


def per_device(rhs, coords, nugget, near_ids, basis):
    vmem = pl.BlockSpec(memory_space=pltpu.VMEM)
    state = pltpu.VMEM((NRHS, WIDTH), F32)
    dma = pltpu.SemaphoreType.DMA
    n = ITERS
    scratch = [
        pltpu.VMEM((LEVELS, RANK, WIDTH), F32),
        pltpu.VMEM((LEVELS * RANK, WIDTH), BF16),
        pltpu.VMEM((LEVELS * RANK, WIDTH), BF16),
        pltpu.VMEM((9, LEAF, LEAF), BF16),
        pltpu.VMEM((9, LEAF, LEAF), BF16),
        pltpu.VMEM((WIDTH, 8), F32),
        pltpu.VMEM((2, 3, LEAF), F32),
        pltpu.VMEM((3 * NRHS, WIDTH), BF16),
        pltpu.VMEM((2, 3 * NRHS, LEAF), BF16),
        state,
        state,
        state,
        state,
        pltpu.VMEM((n, 2, NRHS, LEAF), F32),
        pltpu.VMEM((n, 2, 3, NRHS, RANK), F32),
        pltpu.VMEM((n, 2, NRHS, RANK), F32),
        pltpu.VMEM((n, NC - 1, 3, 8, RANK), F32),
        pltpu.VMEM((n, 4, NRHS, RANK), F32),
        pltpu.VMEM((n, 3, 8, RANK), F32),
        pltpu.VMEM((n, NZ - 1, 2, 8, RANK), F32),
        pltpu.VMEM((n, 8, RANK), F32),
        pltpu.VMEM((n, 8, RANK), F32),
        pltpu.VMEM((n, NY - 1, 8, RANK), F32),
        pltpu.VMEM((n, 2, 3, NRHS, RANK), F32),
        pltpu.VMEM((n + 1, 3, 1, RANK), F32),
        pltpu.VMEM((n + 1, NC + NZ + NY - 3, 1, RANK), F32),
        dma((LEVELS,)),
        dma((2,)),
        dma((n, 2)),
        dma((n,)),
        dma((n,)),
        dma((n,)),
        dma((n,)),
        dma((n,)),
        dma((n,)),
        dma((n,)),
        dma((n + 1, 3)),
        dma((2,)),
        dma((n, 2)),
        dma((n,)),
        dma((n,)),
        dma((n,)),
        dma((n,)),
        dma((n,)),
        dma((n,)),
        dma((n,)),
        dma((n + 1, 3)),
    ]
    return pl.pallas_call(
        kernel,
        out_shape=[jax.ShapeDtypeStruct((NRHS, WIDTH), F32)] * 2,
        in_specs=[
            vmem,
            vmem,
            vmem,
            pl.BlockSpec(memory_space=pltpu.SMEM),
            pl.BlockSpec(memory_space=pl.ANY),
        ],
        out_specs=[vmem, vmem],
        scratch_shapes=scratch,
        compiler_params=pltpu.CompilerParams(
            collective_id=0, has_side_effects=True, vmem_limit_bytes=56 * 1024 * 1024
        ),
    )(rhs, coords, nugget.reshape(1, WIDTH), near_ids, basis)


def solution(mesh):
    placed = (
        P(None, ("row", "col")),
        P(None, ("row", "col")),
        P(("row", "col")),
        P(("row", "col"), None),
        P(None, None, ("row", "col")),
    )
    return jax.shard_map(
        per_device,
        mesh=mesh,
        in_specs=placed,
        out_specs=(P(None, ("row", "col")), P(None, ("row", "col"))),
        check_vma=False,
    )
```

```python
import functools

import jax
import jax.numpy as jnp
from jax import lax
from jax.experimental import pallas as pl
from jax.experimental.pallas import tpu as pltpu
from jax.sharding import PartitionSpec as P

LEAF = 512
ITERS = 4
RANK = 128
NRHS = 32
LEVELS = 10
LEAVES = 4
WIDTH = LEAF * LEAVES
NC, NZ, NY = 8, 8, 4
NDEV = NC * NZ * NY
MESH = pl.DeviceIdType.MESH
F32 = jnp.float32
BF16 = jnp.bfloat16

ROOT_THREE = 1.7320508075688772
LENGTH = 1.6 * LEAF ** (-1.0 / 3.0)
LOG2E = 1.4426950408889634
SCALE = ROOT_THREE / LENGTH * LOG2E


def dot_nn(a, b):
    return lax.dot_general(a, b, (((1,), (0,)), ((), ())), preferred_element_type=F32)


def dot_nt(a, b):
    return lax.dot_general(a, b, (((1,), (1,)), ((), ())), preferred_element_type=F32)


def thirds(value):
    first = value.astype(BF16)
    rest = value - first.astype(F32)
    second = rest.astype(BF16)
    third = (rest - second.astype(F32)).astype(BF16)
    return first, second, third


def split3(value):
    return jnp.concatenate(thirds(value), axis=0)


def product(dot, pieces, high, low):
    rows = pieces.shape[0] // 3
    big = dot(pieces, high)
    small = dot(pieces[: 2 * rows], low)
    return (big[:rows] + (big[rows : 2 * rows] + small[:rows])) + (big[2 * rows :] + small[rows:])


def ring(distance, count):
    return min(distance, count - distance)


FAR = sorted(
    [(j, k) for j in range(NY) for k in range(NZ) if j + k > 0],
    key=lambda jk: (-ring(jk[0], NY) - ring(jk[1], NZ), jk),
)
LINES = (NC - 1) + len(FAR)


def kernel(
    rhs_hbm,
    coords_hbm,
    nugget_hbm,
    ids_ref,
    basis_ref,
    sol_ref,
    res_ref,
    stage,
    bh,
    bl,
    th,
    tl,
    cext,
    nugget_ref,
    chalo,
    fs,
    dirn,
    wvec,
    qvec,
    zvec,
    halo,
    prs,
    p01,
    recv_top,
    recv_low,
    recv01,
    twin_send,
    recv_twin,
    recv_z,
    ysend,
    recv_y,
    tfull,
    scs,
    scr,
    bsem,
    isem,
    csem,
    hsem,
    s_top,
    s_low,
    s01,
    s_twin,
    s_z,
    s_y,
    sg1,
    sg2,
    ssc,
    cs_send,
    hs_send,
    s_top_send,
    s_low_send,
    s01_send,
    s_twin_send,
    s_z_send,
    s_y_send,
    sg1_send,
    sg2_send,
    ssc_send,
):
    row = lax.axis_index("row")
    col = lax.axis_index("col")
    yy = row // NZ
    zz = row % NZ
    hh = col // 4
    gg = col % 4
    dev = row * NC + col
    right_dev = (dev + 1) % NDEV
    left_dev = (dev + NDEV - 1) % NDEV
    right = (right_dev // NC, right_dev % NC)
    left = (left_dev // NC, left_dev % NC)
    cpeers = [(row, (col + k) % NC) for k in range(1, NC)]
    zpeers = [(yy * NZ + (zz + k) % NZ, col) for k in range(1, NZ)]
    ypeers = [(((yy + k) % NY) * NZ + zz, col) for k in range(1, NY)]
    fpeers = [(((yy + j) % NY) * NZ + (zz + k) % NZ, col) for j, k in FAR]
    quad = [(row, (col // 4) * 4 + (col % 4 + k) % 4) for k in range(1, 4)]
    core = (row, col + 1 - 2 * (col % 2))
    twin = (yy * NZ + zz + 1 - 2 * (zz % 2), col)
    my_rows = pl.ds(pl.multiple_of(gg * 8, 8), 8)

    loads = [
        pltpu.make_async_copy(rhs_hbm, qvec, isem.at[0]),
        pltpu.make_async_copy(coords_hbm, cext.at[:, LEAF : LEAF + WIDTH], isem.at[1]),
        pltpu.make_async_copy(nugget_hbm, nugget_ref, isem.at[2]),
    ]
    loads[0].start()
    for level in (8, 9, 6, 7, 4, 5, 2, 3, 0, 1):
        pltpu.make_async_copy(basis_ref.at[level], stage.at[level], bsem.at[level]).start()
    loads[1].start()
    loads[2].start()
    barrier = pltpu.get_barrier_semaphore()
    greeted = fpeers + cpeers + [left, right]
    for peer in greeted:
        pl.semaphore_signal(barrier, inc=1, device_id=peer, device_id_type=MESH)

    def send(src, dst, send_sem, recv_sem, peer):
        pltpu.make_async_remote_copy(
            src_ref=src, dst_ref=dst, send_sem=send_sem, recv_sem=recv_sem, device_id=peer, device_id_type=MESH
        ).start()

    def await_bytes(ref, sem):
        pltpu.make_async_copy(ref, ref, sem).wait()

    lane = lax.broadcasted_iota(jnp.int32, (NRHS, 128), 1)
    sub = lax.broadcasted_iota(jnp.int32, (NRHS, 128), 0)
    hit = (lane % NRHS) == sub

    def as_row(columns):
        spread = jnp.zeros((NRHS, 128), F32)
        for index, column in enumerate(columns):
            spread = jnp.where(hit & (lane // NRHS == index), column, spread)
        return jnp.sum(spread, axis=0, keepdims=True)

    def as_columns(line):
        wide = jnp.where(hit, jnp.broadcast_to(line, (NRHS, 128)), 0.0)
        return [
            jnp.sum(jnp.where(lane // NRHS == index, wide, 0.0), axis=1, keepdims=True)
            for index in range(4)
        ]

    def dots_row():
        r, d, q = res_ref[...], dirn[...], qvec[...]
        return as_row(
            [
                jnp.sum(r * r, axis=1, keepdims=True),
                jnp.sum(d * q, axis=1, keepdims=True),
                jnp.sum(r * q, axis=1, keepdims=True),
                jnp.sum(q * q, axis=1, keepdims=True),
            ]
        )

    def scalar_send(a, phase, peers, base):
        for k, peer in enumerate(peers):
            send(scs.at[a, phase], scr.at[a, base + k], ssc_send.at[a, phase], ssc.at[a, phase], peer)

    def scalar_gather(a, phase, count, base):
        await_bytes(scr.at[a, pl.ds(base, count)], ssc.at[a, phase])
        total = scs[a, phase]
        for k in range(count):
            total = total + scr[a, base + k]
        return total

    def load_levels(levels):
        for level in levels:
            pltpu.make_async_copy(basis_ref.at[level], stage.at[level], bsem.at[level]).wait()
            value = stage[level]
            rows = slice(level * RANK, (level + 1) * RANK)
            high = value.astype(BF16)
            bh[rows, :] = high
            bl[rows, :] = (value - high.astype(F32)).astype(BF16)

    def own(start, width):
        return fs[:, LEAF + start : LEAF + start + width]

    def skeleton_pair(a, level):
        rows = slice(level * RANK, (level + 2) * RANK)
        both = product(dot_nt, own(0, WIDTH), bh[rows, :], bl[rows, :])
        for side in range(2):
            part = both[:, side * RANK : (side + 1) * RANK]
            if level == 2:
                p01[a, side] = part
            else:
                prs[a, side, (level - 4) // 2] = part

    def scaled_pieces(levels, total):
        scaled = jnp.concatenate([t * (1.0 / (LEAF * 2 ** (level + 1))) for level, t in zip(levels, total)], axis=1)
        return split3(scaled), slice(levels[0] * RANK, (levels[-1] + 1) * RANK)

    def spread(levels, total):
        pieces, rows = scaled_pieces(levels, total)
        for start in range(0, WIDTH, 512):
            span = slice(start, start + 512)
            zvec[:, span] += product(dot_nn, pieces, bh[rows, span], bl[rows, span])

    def local_levels():
        for level, cluster in ((0, 2 * LEAF), (1, 4 * LEAF)):
            rows = slice(level * RANK, (level + 1) * RANK)
            for start in range(0, WIDTH, cluster):
                span = slice(start, start + cluster)
                skeleton = product(dot_nt, own(start, cluster), bh[rows, span], bl[rows, span])
                pieces = split3(skeleton * (1.0 / cluster))
                zvec[:, span] += product(dot_nn, pieces, bh[rows, span], bl[rows, span])

    def mask_value(leaf, offset):
        target = dev * LEAVES + leaf + offset - 1
        found = (ids_ref[leaf, 0] == target) | (ids_ref[leaf, 1] == target) | (ids_ref[leaf, 2] == target)
        return jnp.where(found & (target >= 0), 1.0, 0.0).astype(F32)

    def near(leaf):
        span = slice(leaf * LEAF, (leaf + 1) * LEAF)
        window = fs[:, leaf * LEAF : (leaf + 3) * LEAF]
        zvec[:, span] += product(dot_nn, window, th[leaf], tl[leaf])

    def take_halo(a, side):
        await_bytes(halo.at[a, side], hsem.at[a, side])
        start = side * (LEAF + WIDTH)
        fs[:, start : start + LEAF] = split3(halo[a, side])

    def center(leaf):
        first = cext[:, LEAF * (leaf + 1) : LEAF * (leaf + 1) + 128]
        return jnp.floor(first[:, 0:1]) + 0.5

    def features(points):
        parts = [part.astype(F32) for part in thirds(points)]
        norm = jnp.sum(points * points, axis=0, keepdims=True)
        return parts, [part.astype(F32) for part in thirds(norm)]

    def build(leaf):
        middle = center(leaf)
        (one, two, three), norms = features((cext[:, LEAF * (leaf + 1) : LEAF * (leaf + 2)] - middle) * SCALE)
        ones = jnp.ones((3, LEAF), F32)
        blank = jnp.zeros((8, LEAF), F32)
        here = jnp.concatenate([one, two, one, two, three, one], axis=0) * -2.0
        here = jnp.concatenate([here, ones] + norms + [blank], axis=0).astype(BF16)

        def block(offset, carry):
            start = pl.multiple_of((leaf + offset) * LEAF, LEAF)
            (one, two, three), norms = features((cext[:, pl.ds(start, LEAF)] - middle) * SCALE)
            there = jnp.concatenate([one, one, two, two, one, three] + norms + [ones, blank], axis=0)
            square = dot_nn(jnp.transpose(there).astype(BF16), here)
            square = jnp.maximum(square, 1e-30)
            dist = square * lax.rsqrt(square)
            weight = mask_value(leaf, offset) * (1.0 / 48.0)
            value = (weight + (weight * (1.0 / LOG2E)) * dist) * jnp.exp2(-dist)
            high = value.astype(BF16)
            rows = pl.ds(pl.multiple_of(offset * LEAF, LEAF), LEAF)
            th[leaf, rows, :] = high
            tl[leaf, rows, :] = (value - high.astype(F32)).astype(BF16)
            return carry

        lax.fori_loop(0, 3, block, 0)

    def eighth(k):
        other = (col + k) % NC
        return other // 4, pl.ds(pl.multiple_of((other % 4) * 8, 8), 8)

    def apply(a, first):
        if first:
            for level in (8, 6, 4, 2):
                load_levels([level, level + 1])
                skeleton_pair(a, level)
            pl.semaphore_wait(barrier, len(greeted))
        else:
            skeleton_pair(a, 8)
            skeleton_pair(a, 6)
        for k in range(1, NC):
            half, rows = eighth(k)
            part = prs.at[a, half, pl.ds(1, 2), rows, :]
            send(part, recv_top.at[a, k - 1], s_top_send.at[a], s_top.at[a], cpeers[k - 1])
        if not first:
            scs[a, 0] = dots_row()
            scalar_send(a, 0, cpeers, 0)
            skeleton_pair(a, 4)
        for k in range(1, NC):
            half, rows = eighth(k)
            send(prs.at[a, half, 0, rows, :], recv_low.at[a, k - 1], s_low_send.at[a], s_low.at[a], cpeers[k - 1])
        send(qvec.at[:, 0:LEAF], halo.at[a, 1], hs_send.at[a, 1], hsem.at[a, 1], left)
        send(qvec.at[:, WIDTH - LEAF : WIDTH], halo.at[a, 0], hs_send.at[a, 0], hsem.at[a, 0], right)
        if first:
            loads[1].wait()
            loads[2].wait()
            send(cext.at[:, LEAF : 2 * LEAF], chalo.at[1], cs_send.at[1], csem.at[1], left)
            send(cext.at[:, WIDTH : WIDTH + LEAF], chalo.at[0], cs_send.at[0], csem.at[0], right)
        else:
            skeleton_pair(a, 2)
        send(p01.at[a, 0], recv01.at[a, 0], s01_send.at[a], s01.at[a], core)
        for k in range(3):
            send(p01.at[a, 1], recv01.at[a, k + 1], s01_send.at[a], s01.at[a], quad[k])

        def edge(side):
            leaf = side * (LEAVES - 1)
            if first:
                await_bytes(chalo.at[side], csem.at[side])
                start = side * (LEAF + WIDTH)
                cext[:, start : start + LEAF] = chalo[side]
                build(leaf)
            take_halo(a, side)
            near(leaf)

        zvec[...] = nugget_ref[...] * qvec[...]
        if first:
            build(1)
        near(1)

        await_bytes(recv_top.at[a], s_top.at[a])
        for t in range(2):
            total = prs[a, hh, t + 1, my_rows, :]
            for k in range(NC - 1):
                total = total + recv_top[a, k, t]
            ysend[a, t] = total
        for n, (j, k) in enumerate(FAR):
            if j == 0:
                send(ysend.at[a], recv_z.at[a, k - 1], s_z_send.at[a], s_z.at[a], fpeers[n])
            else:
                slot = (j - 1) * NZ + k
                send(ysend.at[a, 1], recv_y.at[a, slot], s_y_send.at[a], s_y.at[a], fpeers[n])
        if not first:
            scs[a, 1] = scalar_gather(a, 0, NC - 1, 0)
            scalar_send(a, 1, zpeers, NC - 1)
        await_bytes(recv_low.at[a], s_low.at[a])
        total = prs[a, hh, 0, my_rows, :]
        for k in range(NC - 1):
            total = total + recv_low[a, k]
        twin_send[a] = total
        send(twin_send.at[a], recv_twin.at[a], s_twin_send.at[a], s_twin.at[a], twin)

        if first:
            build(2)
        near(2)
        edge(0)
        if not first:
            edge(1)
        await_bytes(recv_twin.at[a], s_twin.at[a])
        tfull[a, hh, 0, my_rows, :] = twin_send[a] + hh.astype(F32) * recv_twin[a]
        mine = tfull.at[a, hh, 0, my_rows, :]
        for k in range(1, NC):
            send(mine, mine, sg1_send.at[a], sg1.at[a], cpeers[k - 1])
        if first:
            load_levels([0, 1])
        local_levels()
        if not first:
            scs[a, 2] = scalar_gather(a, 1, NZ - 1, NC - 1)
            scalar_send(a, 2, ypeers, NC + NZ - 2)

        await_bytes(recv_z.at[a], s_z.at[a])
        await_bytes(recv_y.at[a], s_y.at[a])
        one = ysend[a, 0]
        two = ysend[a, 1]
        for k in range(1, NZ):
            source = (zz + NZ - k) % NZ
            quarter = jnp.where((hh == 1) | (source // 4 == zz // 4), 1.0, 0.0).astype(F32)
            one = one + quarter * recv_z[a, k - 1, 0]
            two = two + recv_z[a, k - 1, 1]
        for j in range(1, NY):
            source = (yy + NY - j) % NY
            half = jnp.where((hh == 1) | (source // 2 == yy // 2), 1.0, 0.0).astype(F32)
            ring_sum = recv_y[a, (j - 1) * NZ]
            for k in range(1, NZ):
                ring_sum = ring_sum + recv_y[a, (j - 1) * NZ + k]
            two = two + half * ring_sum
        tfull[a, hh, 1, my_rows, :] = one
        tfull[a, hh, 2, my_rows, :] = two
        mine = tfull.at[a, hh, pl.ds(1, 2), my_rows, :]
        for k in range(1, NC):
            send(mine, mine, sg2_send.at[a], sg2.at[a], cpeers[k - 1])

        if first:
            edge(1)
        await_bytes(recv01.at[a], s01.at[a])
        pair = p01[a, 0] + recv01[a, 0]
        four = (p01[a, 1] + recv01[a, 1]) + (recv01[a, 2] + recv01[a, 3])
        await_bytes(recv_low.at[a], sg1.at[a])
        spread(list(range(2, 6)), [pair, four, tfull[a, 0, 0], tfull[a, 1, 0]])
        await_bytes(halo.at[a, 0], hs_send.at[a, 0])
        await_bytes(halo.at[a, 1], hs_send.at[a, 1])

    def top_levels(a, finish):
        await_bytes(recv_top.at[a], sg2.at[a])
        levels = [tfull[a, 0, 1], tfull[a, 1, 1], tfull[a, 0, 2], tfull[a, 1, 2]]
        pieces, rows = scaled_pieces(list(range(6, 10)), levels)
        for start in range(0, WIDTH, 512):
            span = slice(start, start + 512)
            q = finish(span, product(dot_nn, pieces, bh[rows, span], bl[rows, span]))
            qvec[:, span] = q
            fs[:, LEAF + start : LEAF + start + 512] = split3(q)

    def steps(total):
        norm, curve, cross, square = as_columns(total)
        step = norm / curve
        fresh = jnp.maximum(norm - 2.0 * step * cross + step * step * square, 0.0)
        return step, fresh / norm

    loads[0].wait()
    start = qvec[...]
    fs[:, LEAF : LEAF + WIDTH] = split3(start)
    sol_ref[...] = jnp.zeros_like(sol_ref)
    res_ref[...] = start
    dirn[...] = start
    apply(0, True)

    def first_image(span, top):
        image = zvec[:, span] + top
        wvec[:, span] = image
        return image

    top_levels(0, first_image)

    def iteration(a, carry):
        apply(a, False)
        step, ratio = steps(scalar_gather(a, 2, NY - 1, NC + NZ - 2))
        q = qvec[...]
        d = dirn[...]
        sol_ref[...] += step * d
        r = res_ref[...] - step * q
        res_ref[...] = r
        dirn[...] = r + ratio * d
        w = wvec[...] - step * zvec[...]
        wvec[...] = w
        qvec[...] = w + ratio * q

        def next_image(span, top):
            change = step * top
            wvec[:, span] -= change
            return qvec[:, span] - change

        top_levels(a, next_image)
        return carry

    lax.fori_loop(1, ITERS, iteration, 0)

    last = ITERS
    scs[last, 0] = dots_row()
    scalar_send(last, 0, cpeers, 0)
    scs[last, 1] = scalar_gather(last, 0, NC - 1, 0)
    scalar_send(last, 1, fpeers, NC - 1)
    step, _ = steps(scalar_gather(last, 1, len(FAR), NC - 1))
    sol_ref[...] += step * dirn[...]
    res_ref[...] += -step * qvec[...]

    def drain(a, carry):
        await_bytes(recv_top.at[a], s_top_send.at[a])
        await_bytes(recv_low.at[a], s_low_send.at[a])
        await_bytes(recv01.at[a], s01_send.at[a])
        await_bytes(recv_twin.at[a], s_twin_send.at[a])
        await_bytes(recv_z.at[a], s_z_send.at[a])
        await_bytes(recv_y.at[a], s_y_send.at[a])
        await_bytes(recv_low.at[a], sg1_send.at[a])
        await_bytes(recv_top.at[a], sg2_send.at[a])
        return carry

    def drain_scalars(a, carry):
        for phase, (base, count) in enumerate(((0, NC - 1), (NC - 1, NZ - 1), (NC + NZ - 2, NY - 1))):
            await_bytes(scr.at[a, pl.ds(base, count)], ssc_send.at[a, phase])
        return carry

    lax.fori_loop(0, ITERS, drain, 0)
    lax.fori_loop(1, ITERS, drain_scalars, 0)
    await_bytes(scr.at[last, pl.ds(0, NC - 1)], ssc_send.at[last, 0])
    await_bytes(scr.at[last, pl.ds(NC - 1, len(FAR))], ssc_send.at[last, 1])
    for side in range(2):
        await_bytes(chalo.at[side], cs_send.at[side])


def hand_over(sol_ref, res_ref, sol_out, res_out):
    sol_out[...] = sol_ref[...]
    res_out[...] = res_ref[...]


def per_device(rhs, coords, nugget, near_ids, basis):
    anywhere = pl.BlockSpec(memory_space=pl.ANY)
    vmem = pl.BlockSpec(memory_space=pltpu.VMEM)
    state = pltpu.VMEM((NRHS, WIDTH), F32)
    dma = pltpu.SemaphoreType.DMA
    n = ITERS
    scratch = [
        pltpu.VMEM((LEVELS, RANK, WIDTH), F32),
        pltpu.VMEM((LEVELS * RANK, WIDTH), BF16),
        pltpu.VMEM((LEVELS * RANK, WIDTH), BF16),
        pltpu.VMEM((LEAVES, 3 * LEAF, LEAF), BF16),
        pltpu.VMEM((LEAVES, 3 * LEAF, LEAF), BF16),
        pltpu.VMEM((3, WIDTH + 2 * LEAF), F32),
        pltpu.VMEM((1, WIDTH), F32),
        pltpu.VMEM((2, 3, LEAF), F32),
        pltpu.VMEM((3 * NRHS, WIDTH + 2 * LEAF), BF16),
        state,
        state,
        state,
        state,
        pltpu.VMEM((n, 2, NRHS, LEAF), F32),
        pltpu.VMEM((n, 2, 3, NRHS, RANK), F32),
        pltpu.VMEM((n, 2, NRHS, RANK), F32),
        pltpu.VMEM((n, NC - 1, 2, 8, RANK), F32),
        pltpu.VMEM((n, NC - 1, 8, RANK), F32),
        pltpu.VMEM((n, 4, NRHS, RANK), F32),
        pltpu.VMEM((n, 8, RANK), F32),
        pltpu.VMEM((n, 8, RANK), F32),
        pltpu.VMEM((n, NZ - 1, 2, 8, RANK), F32),
        pltpu.VMEM((n, 2, 8, RANK), F32),
        pltpu.VMEM((n, NZ * (NY - 1), 8, RANK), F32),
        pltpu.VMEM((n, 2, 3, NRHS, RANK), F32),
        pltpu.VMEM((n + 1, 3, 1, RANK), F32),
        pltpu.VMEM((n + 1, LINES, 1, RANK), F32),
        dma((LEVELS,)),
        dma((3,)),
        dma((2,)),
        dma((n, 2)),
        dma((n,)),
        dma((n,)),
        dma((n,)),
        dma((n,)),
        dma((n,)),
        dma((n,)),
        dma((n,)),
        dma((n,)),
        dma((n + 1, 3)),
        dma((2,)),
        dma((n, 2)),
        dma((n,)),
        dma((n,)),
        dma((n,)),
        dma((n,)),
        dma((n,)),
        dma((n,)),
        dma((n,)),
        dma((n,)),
        dma((n + 1, 3)),
    ]
    field = jax.ShapeDtypeStruct((NRHS, WIDTH), F32)
    parts = pl.pallas_call(
        kernel,
        out_shape=[field] * 2,
        in_specs=[anywhere, anywhere, anywhere, pl.BlockSpec(memory_space=pltpu.SMEM), anywhere],
        out_specs=[vmem, vmem],
        scratch_shapes=scratch,
        compiler_params=pltpu.CompilerParams(
            collective_id=0, has_side_effects=True, vmem_limit_bytes=56 * 1024 * 1024
        ),
    )(rhs, coords, nugget.reshape(1, WIDTH), near_ids, basis)
    return tuple(
        pl.pallas_call(
            hand_over,
            out_shape=[field] * 2,
            in_specs=[vmem] * 2,
            out_specs=[vmem] * 2,
        )(*parts)
    )


def solution(mesh):
    placed = (
        P(None, ("row", "col")),
        P(None, ("row", "col")),
        P(("row", "col")),
        P(("row", "col"), None),
        P(None, None, ("row", "col")),
    )
    return jax.shard_map(
        per_device,
        mesh=mesh,
        in_specs=placed,
        out_specs=(P(None, ("row", "col")), P(None, ("row", "col"))),
        check_vma=False,
    )
```

```python
import functools

import jax
import jax.numpy as jnp
from jax import lax
from jax.experimental import pallas as pl
from jax.experimental.pallas import tpu as pltpu
from jax.sharding import PartitionSpec as P

LEAF = 512
ITERS = 4
RANK = 128
NRHS = 32
LEVELS = 10
LEAVES = 4
WIDTH = LEAF * LEAVES
NC, NZ, NY = 8, 8, 4
NDEV = NC * NZ * NY
MESH = pl.DeviceIdType.MESH
F32 = jnp.float32
BF16 = jnp.bfloat16

ROOT_THREE = 1.7320508075688772
LENGTH = 1.6 * LEAF ** (-1.0 / 3.0)
LOG2E = 1.4426950408889634
SCALE = ROOT_THREE / LENGTH * LOG2E


def dot_nn(a, b):
    return lax.dot_general(a, b, (((1,), (0,)), ((), ())), preferred_element_type=F32)


def thirds(value):
    first = value.astype(BF16)
    rest = value - first.astype(F32)
    second = rest.astype(BF16)
    third = (rest - second.astype(F32)).astype(BF16)
    return first, second, third


def split3(value):
    return jnp.concatenate(thirds(value), axis=0)


def product(dot, pieces, high, low):
    rows = pieces.shape[0] // 3
    big = dot(pieces, high)
    small = dot(pieces[: 2 * rows], low)
    return (big[:rows] + (big[rows : 2 * rows] + small[:rows])) + (big[2 * rows :] + small[rows:])


def ring(distance, count):
    return min(distance, count - distance)


FAR = sorted(
    [(j, k) for j in range(NY) for k in range(NZ) if j + k > 0],
    key=lambda jk: (-ring(jk[0], NY) - ring(jk[1], NZ), jk),
)
COL_ORDER = (4, 5, 3, 2, 6, 7, 1)
Z_ORDER = (4, 3, 5, 2, 6, 1, 7)
LINES = (NC - 1) + len(FAR)


def kernel(
    rhs_hbm,
    coords_hbm,
    nugget_hbm,
    ids_ref,
    basis_ref,
    sol_ref,
    res_ref,
    stage,
    bh,
    bl,
    bth,
    btl,
    th,
    tl,
    cext,
    nugget_ref,
    chalo,
    fs,
    dirn,
    wvec,
    qvec,
    zvec,
    halo,
    prs,
    p01,
    recv_top,
    recv_low,
    recv01,
    twin_send,
    recv_twin,
    recv_z,
    ysend,
    recv_y,
    tfull,
    scs,
    scr,
    gate,
    bsem,
    isem,
    csem,
    hsem,
    s_top,
    s_low,
    s01,
    s_twin,
    s_z,
    s_y,
    sg1,
    sg2,
    ssc,
    cs_send,
    hs_send,
    s_top_send,
    s_low_send,
    s01_send,
    s_twin_send,
    s_z_send,
    s_y_send,
    sg1_send,
    sg2_send,
    ssc_send,
):
    row = lax.axis_index("row")
    col = lax.axis_index("col")
    yy = row // NZ
    zz = row % NZ
    hh = col // 4
    gg = col % 4
    dev = row * NC + col
    right_dev = (dev + 1) % NDEV
    left_dev = (dev + NDEV - 1) % NDEV
    right = (right_dev // NC, right_dev % NC)
    left = (left_dev // NC, left_dev % NC)
    cpeers = [(row, (col + k) % NC) for k in range(1, NC)]
    zpeers = [(yy * NZ + (zz + k) % NZ, col) for k in range(1, NZ)]
    ypeers = [(((yy + k) % NY) * NZ + zz, col) for k in range(1, NY)]
    fpeers = [(((yy + j) % NY) * NZ + (zz + k) % NZ, col) for j, k in FAR]
    quad = [(row, (col // 4) * 4 + (col % 4 + k) % 4) for k in range(1, 4)]
    core = (row, col + 1 - 2 * (col % 2))
    twin = (yy * NZ + zz + 1 - 2 * (zz % 2), col)
    my_rows = pl.ds(pl.multiple_of(gg * 8, 8), 8)

    loads = [
        pltpu.make_async_copy(rhs_hbm, qvec, isem.at[0]),
        pltpu.make_async_copy(coords_hbm, cext.at[:, LEAF : LEAF + WIDTH], isem.at[1]),
        pltpu.make_async_copy(nugget_hbm, nugget_ref, isem.at[2]),
    ]
    loads[0].start()
    for level in (8, 9, 6, 7, 4, 5, 2, 3, 0, 1):
        pltpu.make_async_copy(basis_ref.at[level], stage.at[level], bsem.at[level]).start()
    loads[1].start()
    loads[2].start()
    barrier = pltpu.get_barrier_semaphore()
    greeted = zpeers + cpeers + ypeers + [left, right]
    for peer in greeted:
        pl.semaphore_signal(barrier, inc=1, device_id=peer, device_id_type=MESH)

    def send(src, dst, send_sem, recv_sem, peer):
        pltpu.make_async_remote_copy(
            src_ref=src, dst_ref=dst, send_sem=send_sem, recv_sem=recv_sem, device_id=peer, device_id_type=MESH
        ).start()

    def await_bytes(ref, sem):
        pltpu.make_async_copy(ref, ref, sem).wait()

    lane = lax.broadcasted_iota(jnp.int32, (NRHS, 128), 1)
    sub = lax.broadcasted_iota(jnp.int32, (NRHS, 128), 0)
    hit = (lane % NRHS) == sub

    def as_row(columns):
        spread = jnp.zeros((NRHS, 128), F32)
        for index, column in enumerate(columns):
            spread = jnp.where(hit & (lane // NRHS == index), column, spread)
        return jnp.sum(spread, axis=0, keepdims=True)

    def as_columns(line):
        wide = jnp.where(hit, jnp.broadcast_to(line, (NRHS, 128)), 0.0)
        return [
            jnp.sum(jnp.where(lane // NRHS == index, wide, 0.0), axis=1, keepdims=True)
            for index in range(4)
        ]

    def dots_row():
        r, d, q = res_ref[...], dirn[...], qvec[...]
        return as_row(
            [
                jnp.sum(r * r, axis=1, keepdims=True),
                jnp.sum(d * q, axis=1, keepdims=True),
                jnp.sum(r * q, axis=1, keepdims=True),
                jnp.sum(q * q, axis=1, keepdims=True),
            ]
        )

    def scalar_send(a, phase, peers, base):
        order = {NC - 1: COL_ORDER if phase == 0 else Z_ORDER}.get(len(peers), range(1, len(peers) + 1))
        for k in order:
            send(scs.at[a, phase], scr.at[a, base + k - 1], ssc_send.at[a, phase], ssc.at[a, phase], peers[k - 1])

    def scalar_gather(a, phase, count, base):
        await_bytes(scr.at[a, pl.ds(base, count)], ssc.at[a, phase])
        total = scs[a, phase]
        for k in range(count):
            total = total + scr[a, base + k]
        return total

    def load_levels(levels):
        for level in levels:
            pltpu.make_async_copy(basis_ref.at[level], stage.at[level], bsem.at[level]).wait()
            rows = slice(level * RANK, (level + 1) * RANK)
            value = stage[level]
            high = value.astype(BF16)
            bh[rows, :] = high
            bl[rows, :] = (value - high.astype(F32)).astype(BF16)
            value = jnp.transpose(stage[level])
            high = value.astype(BF16)
            bth[:, rows] = high
            btl[:, rows] = (value - high.astype(F32)).astype(BF16)

    def own(start, width):
        return fs[:, LEAF + start : LEAF + start + width]

    def skeleton_pair(a, level):
        rows = slice(level * RANK, (level + 2) * RANK)
        both = product(dot_nn, own(0, WIDTH), bth[:, rows], btl[:, rows])
        for side in range(2):
            part = both[:, side * RANK : (side + 1) * RANK]
            if level == 2:
                p01[a, side] = part
            else:
                prs[a, side, (level - 4) // 2] = part

    def scaled_pieces(levels, total):
        scaled = jnp.concatenate([t * (1.0 / (LEAF * 2 ** (level + 1))) for level, t in zip(levels, total)], axis=1)
        return split3(scaled), slice(levels[0] * RANK, (levels[-1] + 1) * RANK)

    def spread(levels, total):
        pieces, rows = scaled_pieces(levels, total)
        for start in range(0, WIDTH, 512):
            span = slice(start, start + 512)
            zvec[:, span] += product(dot_nn, pieces, bh[rows, span], bl[rows, span])

    def local_levels():
        rows = slice(0, 2 * RANK)
        half = WIDTH // 2
        spans = [slice(0, half), slice(half, WIDTH)]
        parts = [product(dot_nn, own(span.start, half), bth[span, rows], btl[span, rows]) for span in spans]
        whole = (parts[0][:, RANK:] + parts[1][:, RANK:]) * (1.0 / WIDTH)
        for span, part in zip(spans, parts):
            pieces = split3(jnp.concatenate([part[:, :RANK] * (1.0 / half), whole], axis=1))
            zvec[:, span] += product(dot_nn, pieces, bh[rows, span], bl[rows, span])

    def mask_value(leaf, offset):
        target = dev * LEAVES + leaf + offset - 1
        found = (ids_ref[leaf, 0] == target) | (ids_ref[leaf, 1] == target) | (ids_ref[leaf, 2] == target)
        return jnp.where(found & (target >= 0), 1.0, 0.0).astype(F32)

    def near(leaf):
        span = slice(leaf * LEAF, (leaf + 1) * LEAF)
        window = fs[:, leaf * LEAF : (leaf + 3) * LEAF]
        zvec[:, span] += product(dot_nn, window, th[leaf], tl[leaf])

    def take_halo(a, side):
        await_bytes(halo.at[a, side], hsem.at[a, side])
        start = side * (LEAF + WIDTH)
        fs[:, start : start + LEAF] = split3(halo[a, side])

    def center(leaf):
        first = cext[:, LEAF * (leaf + 1) : LEAF * (leaf + 1) + 128]
        return jnp.floor(first[:, 0:1]) + 0.5

    def features(points):
        parts = [part.astype(F32) for part in thirds(points)]
        norm = jnp.sum(points * points, axis=0, keepdims=True)
        return parts, [part.astype(F32) for part in thirds(norm)]

    def build(leaf):
        middle = center(leaf)
        (one, two, three), norms = features((cext[:, LEAF * (leaf + 1) : LEAF * (leaf + 2)] - middle) * SCALE)
        ones = jnp.ones((3, LEAF), F32)
        blank = jnp.zeros((8, LEAF), F32)
        here = jnp.concatenate([one, two, one, two, three, one], axis=0) * -2.0
        here = jnp.concatenate([here, ones] + norms + [blank], axis=0).astype(BF16)

        def block(offset, carry):
            start = pl.multiple_of((leaf + offset) * LEAF, LEAF)
            (one, two, three), norms = features((cext[:, pl.ds(start, LEAF)] - middle) * SCALE)
            there = jnp.concatenate([one, one, two, two, one, three] + norms + [ones, blank], axis=0)
            square = dot_nn(jnp.transpose(there).astype(BF16), here)
            square = jnp.maximum(square, 1e-30)
            dist = square * lax.rsqrt(square)
            weight = mask_value(leaf, offset) * (1.0 / 48.0)
            value = (weight + (weight * (1.0 / LOG2E)) * dist) * jnp.exp2(-dist)
            high = value.astype(BF16)
            rows = pl.ds(pl.multiple_of(offset * LEAF, LEAF), LEAF)
            th[leaf, rows, :] = high
            tl[leaf, rows, :] = (value - high.astype(F32)).astype(BF16)
            return carry

        lax.fori_loop(0, 3, block, 0)

    def eighth(k):
        other = (col + k) % NC
        return other // 4, pl.ds(pl.multiple_of((other % 4) * 8, 8), 8)

    def apply(a, first):
        if first:
            load_levels([8, 9, 6, 7])
            skeleton_pair(a, 8)
            skeleton_pair(a, 6)
            pl.semaphore_wait(barrier, len(greeted))
        else:
            skeleton_pair(a, 8)
            skeleton_pair(a, 6)
        for k in COL_ORDER:
            half, rows = eighth(k)
            part = prs.at[a, half, pl.ds(1, 2), rows, :]
            send(part, recv_top.at[a, k - 1], s_top_send.at[a], s_top.at[a], cpeers[k - 1])
        if first:
            for peer in ypeers:
                pl.semaphore_signal(gate, inc=1, device_id=peer, device_id_type=MESH)
            load_levels([4, 5])
        else:
            scs[a, 0] = dots_row()
            scalar_send(a, 0, cpeers, 0)
        skeleton_pair(a, 4)
        for k in COL_ORDER:
            half, rows = eighth(k)
            send(prs.at[a, half, 0, rows, :], recv_low.at[a, k - 1], s_low_send.at[a], s_low.at[a], cpeers[k - 1])
        send(qvec.at[:, 0:LEAF], halo.at[a, 1], hs_send.at[a, 1], hsem.at[a, 1], left)
        send(qvec.at[:, WIDTH - LEAF : WIDTH], halo.at[a, 0], hs_send.at[a, 0], hsem.at[a, 0], right)
        if first:
            loads[1].wait()
            loads[2].wait()
            send(cext.at[:, LEAF : 2 * LEAF], chalo.at[1], cs_send.at[1], csem.at[1], left)
            send(cext.at[:, WIDTH : WIDTH + LEAF], chalo.at[0], cs_send.at[0], csem.at[0], right)
            load_levels([2, 3])
        skeleton_pair(a, 2)
        send(p01.at[a, 0], recv01.at[a, 0], s01_send.at[a], s01.at[a], core)
        for k in range(3):
            send(p01.at[a, 1], recv01.at[a, k + 1], s01_send.at[a], s01.at[a], quad[k])

        def edge(side):
            leaf = side * (LEAVES - 1)
            if first:
                await_bytes(chalo.at[side], csem.at[side])
                start = side * (LEAF + WIDTH)
                cext[:, start : start + LEAF] = chalo[side]
                build(leaf)
            take_halo(a, side)
            near(leaf)

        zvec[...] = nugget_ref[...] * qvec[...]
        if first:
            build(1)
        near(1)

        await_bytes(recv_top.at[a], s_top.at[a])
        for t in range(2):
            total = prs[a, hh, t + 1, my_rows, :]
            for k in range(NC - 1):
                total = total + recv_top[a, k, t]
            ysend[a, t] = total
        if first:
            pl.semaphore_wait(gate, len(ypeers))
        for n, (j, k) in enumerate(FAR):
            if j == 0:
                send(ysend.at[a], recv_z.at[a, k - 1], s_z_send.at[a], s_z.at[a], fpeers[n])
            else:
                slot = (j - 1) * NZ + k
                send(ysend.at[a, 1], recv_y.at[a, slot], s_y_send.at[a], s_y.at[a], fpeers[n])
        if not first:
            scs[a, 1] = scalar_gather(a, 0, NC - 1, 0)
            scalar_send(a, 1, zpeers, NC - 1)
        await_bytes(recv_low.at[a], s_low.at[a])
        total = prs[a, hh, 0, my_rows, :]
        for k in range(NC - 1):
            total = total + recv_low[a, k]
        twin_send[a] = total
        send(twin_send.at[a], recv_twin.at[a], s_twin_send.at[a], s_twin.at[a], twin)

        if first:
            build(2)
        near(2)
        edge(0)
        if not first:
            edge(1)
        await_bytes(recv_twin.at[a], s_twin.at[a])
        tfull[a, hh, 0, my_rows, :] = twin_send[a] + hh.astype(F32) * recv_twin[a]
        mine = tfull.at[a, hh, 0, my_rows, :]
        for k in COL_ORDER:
            send(mine, mine, sg1_send.at[a], sg1.at[a], cpeers[k - 1])
        if first:
            load_levels([0, 1])
        local_levels()
        if not first:
            scs[a, 2] = scalar_gather(a, 1, NZ - 1, NC - 1)
            scalar_send(a, 2, ypeers, NC + NZ - 2)

        await_bytes(recv_z.at[a], s_z.at[a])
        await_bytes(recv_y.at[a], s_y.at[a])
        one = ysend[a, 0]
        two = ysend[a, 1]
        for k in range(1, NZ):
            source = (zz + NZ - k) % NZ
            quarter = jnp.where((hh == 1) | (source // 4 == zz // 4), 1.0, 0.0).astype(F32)
            one = one + quarter * recv_z[a, k - 1, 0]
            two = two + recv_z[a, k - 1, 1]
        for j in range(1, NY):
            source = (yy + NY - j) % NY
            half = jnp.where((hh == 1) | (source // 2 == yy // 2), 1.0, 0.0).astype(F32)
            ring_sum = recv_y[a, (j - 1) * NZ]
            for k in range(1, NZ):
                ring_sum = ring_sum + recv_y[a, (j - 1) * NZ + k]
            two = two + half * ring_sum
        tfull[a, hh, 1, my_rows, :] = one
        tfull[a, hh, 2, my_rows, :] = two
        mine = tfull.at[a, hh, pl.ds(1, 2), my_rows, :]
        for k in COL_ORDER:
            send(mine, mine, sg2_send.at[a], sg2.at[a], cpeers[k - 1])

        if first:
            edge(1)
        await_bytes(recv01.at[a], s01.at[a])
        pair = p01[a, 0] + recv01[a, 0]
        four = (p01[a, 1] + recv01[a, 1]) + (recv01[a, 2] + recv01[a, 3])
        await_bytes(recv_low.at[a], sg1.at[a])
        spread(list(range(2, 6)), [pair, four, tfull[a, 0, 0], tfull[a, 1, 0]])
        await_bytes(halo.at[a, 0], hs_send.at[a, 0])
        await_bytes(halo.at[a, 1], hs_send.at[a, 1])

    def top_levels(a, finish):
        await_bytes(recv_top.at[a], sg2.at[a])
        levels = [tfull[a, 0, 1], tfull[a, 1, 1], tfull[a, 0, 2], tfull[a, 1, 2]]
        pieces, rows = scaled_pieces(list(range(6, 10)), levels)
        for start in range(0, WIDTH, 512):
            span = slice(start, start + 512)
            q = finish(span, product(dot_nn, pieces, bh[rows, span], bl[rows, span]))
            qvec[:, span] = q
            fs[:, LEAF + start : LEAF + start + 512] = split3(q)

    def steps(total):
        norm, curve, cross, square = as_columns(total)
        step = norm / curve
        fresh = jnp.maximum(norm - 2.0 * step * cross + step * step * square, 0.0)
        return step, fresh / norm

    loads[0].wait()
    start = qvec[...]
    fs[:, LEAF : LEAF + WIDTH] = split3(start)
    sol_ref[...] = jnp.zeros_like(sol_ref)
    res_ref[...] = start
    dirn[...] = start
    apply(0, True)

    def first_image(span, top):
        image = zvec[:, span] + top
        wvec[:, span] = image
        return image

    top_levels(0, first_image)

    def iteration(a, carry):
        apply(a, False)
        step, ratio = steps(scalar_gather(a, 2, NY - 1, NC + NZ - 2))
        q = qvec[...]
        d = dirn[...]
        sol_ref[...] += step * d
        r = res_ref[...] - step * q
        res_ref[...] = r
        dirn[...] = r + ratio * d
        w = wvec[...] - step * zvec[...]
        wvec[...] = w
        qvec[...] = w + ratio * q

        def next_image(span, top):
            change = step * top
            wvec[:, span] -= change
            return qvec[:, span] - change

        top_levels(a, next_image)
        return carry

    lax.fori_loop(1, ITERS, iteration, 0)

    last = ITERS
    scs[last, 0] = dots_row()
    scalar_send(last, 0, cpeers, 0)
    scs[last, 1] = scalar_gather(last, 0, NC - 1, 0)
    scalar_send(last, 1, fpeers, NC - 1)
    step, _ = steps(scalar_gather(last, 1, len(FAR), NC - 1))
    sol_ref[...] += step * dirn[...]
    res_ref[...] += -step * qvec[...]

    def drain(a, carry):
        await_bytes(recv_top.at[a], s_top_send.at[a])
        await_bytes(recv_low.at[a], s_low_send.at[a])
        await_bytes(recv01.at[a], s01_send.at[a])
        await_bytes(recv_twin.at[a], s_twin_send.at[a])
        await_bytes(recv_z.at[a], s_z_send.at[a])
        await_bytes(recv_y.at[a], s_y_send.at[a])
        await_bytes(recv_low.at[a], sg1_send.at[a])
        await_bytes(recv_top.at[a], sg2_send.at[a])
        return carry

    def drain_scalars(a, carry):
        for phase, (base, count) in enumerate(((0, NC - 1), (NC - 1, NZ - 1), (NC + NZ - 2, NY - 1))):
            await_bytes(scr.at[a, pl.ds(base, count)], ssc_send.at[a, phase])
        return carry

    lax.fori_loop(0, ITERS, drain, 0)
    lax.fori_loop(1, ITERS, drain_scalars, 0)
    await_bytes(scr.at[last, pl.ds(0, NC - 1)], ssc_send.at[last, 0])
    await_bytes(scr.at[last, pl.ds(NC - 1, len(FAR))], ssc_send.at[last, 1])
    for side in range(2):
        await_bytes(chalo.at[side], cs_send.at[side])


def hand_over(sol_ref, res_ref, sol_out, res_out):
    sol_out[...] = sol_ref[...]
    res_out[...] = res_ref[...]


def per_device(rhs, coords, nugget, near_ids, basis):
    anywhere = pl.BlockSpec(memory_space=pl.ANY)
    vmem = pl.BlockSpec(memory_space=pltpu.VMEM)
    state = pltpu.VMEM((NRHS, WIDTH), F32)
    dma = pltpu.SemaphoreType.DMA
    n = ITERS
    scratch = [
        pltpu.VMEM((LEVELS, RANK, WIDTH), F32),
        pltpu.VMEM((LEVELS * RANK, WIDTH), BF16),
        pltpu.VMEM((LEVELS * RANK, WIDTH), BF16),
        pltpu.VMEM((WIDTH, LEVELS * RANK), BF16),
        pltpu.VMEM((WIDTH, LEVELS * RANK), BF16),
        pltpu.VMEM((LEAVES, 3 * LEAF, LEAF), BF16),
        pltpu.VMEM((LEAVES, 3 * LEAF, LEAF), BF16),
        pltpu.VMEM((3, WIDTH + 2 * LEAF), F32),
        pltpu.VMEM((1, WIDTH), F32),
        pltpu.VMEM((2, 3, LEAF), F32),
        pltpu.VMEM((3 * NRHS, WIDTH + 2 * LEAF), BF16),
        state,
        state,
        state,
        state,
        pltpu.VMEM((n, 2, NRHS, LEAF), F32),
        pltpu.VMEM((n, 2, 3, NRHS, RANK), F32),
        pltpu.VMEM((n, 2, NRHS, RANK), F32),
        pltpu.VMEM((n, NC - 1, 2, 8, RANK), F32),
        pltpu.VMEM((n, NC - 1, 8, RANK), F32),
        pltpu.VMEM((n, 4, NRHS, RANK), F32),
        pltpu.VMEM((n, 8, RANK), F32),
        pltpu.VMEM((n, 8, RANK), F32),
        pltpu.VMEM((n, NZ - 1, 2, 8, RANK), F32),
        pltpu.VMEM((n, 2, 8, RANK), F32),
        pltpu.VMEM((n, NZ * (NY - 1), 8, RANK), F32),
        pltpu.VMEM((n, 2, 3, NRHS, RANK), F32),
        pltpu.VMEM((n + 1, 3, 1, RANK), F32),
        pltpu.VMEM((n + 1, LINES, 1, RANK), F32),
        pltpu.SemaphoreType.REGULAR,
        dma((LEVELS,)),
        dma((3,)),
        dma((2,)),
        dma((n, 2)),
        dma((n,)),
        dma((n,)),
        dma((n,)),
        dma((n,)),
        dma((n,)),
        dma((n,)),
        dma((n,)),
        dma((n,)),
        dma((n + 1, 3)),
        dma((2,)),
        dma((n, 2)),
        dma((n,)),
        dma((n,)),
        dma((n,)),
        dma((n,)),
        dma((n,)),
        dma((n,)),
        dma((n,)),
        dma((n,)),
        dma((n + 1, 3)),
    ]
    field = jax.ShapeDtypeStruct((NRHS, WIDTH), F32)
    parts = pl.pallas_call(
        kernel,
        out_shape=[field] * 2,
        in_specs=[anywhere, anywhere, anywhere, pl.BlockSpec(memory_space=pltpu.SMEM), anywhere],
        out_specs=[vmem, vmem],
        scratch_shapes=scratch,
        compiler_params=pltpu.CompilerParams(
            collective_id=0, has_side_effects=True, vmem_limit_bytes=56 * 1024 * 1024
        ),
    )(rhs, coords, nugget.reshape(1, WIDTH), near_ids, basis)
    return tuple(
        pl.pallas_call(
            hand_over,
            out_shape=[field] * 2,
            in_specs=[vmem] * 2,
            out_specs=[vmem] * 2,
        )(*parts)
    )


def solution(mesh):
    placed = (
        P(None, ("row", "col")),
        P(None, ("row", "col")),
        P(("row", "col")),
        P(("row", "col"), None),
        P(None, None, ("row", "col")),
    )
    return jax.shard_map(
        per_device,
        mesh=mesh,
        in_specs=placed,
        out_specs=(P(None, ("row", "col")), P(None, ("row", "col"))),
        check_vma=False,
    )
```

```python
import functools

import jax
import jax.numpy as jnp
from jax import lax
from jax.experimental import pallas as pl
from jax.experimental.pallas import tpu as pltpu
from jax.sharding import PartitionSpec as P

LEAF = 512
ITERS = 4
RANK = 128
NRHS = 32
LEVELS = 10
LEAVES = 4
WIDTH = LEAF * LEAVES
NC, NZ, NY = 8, 8, 4
NDEV = NC * NZ * NY
MESH = pl.DeviceIdType.MESH
F32 = jnp.float32
BF16 = jnp.bfloat16

ROOT_THREE = 1.7320508075688772
LENGTH = 1.6 * LEAF ** (-1.0 / 3.0)
LOG2E = 1.4426950408889634
SCALE = ROOT_THREE / LENGTH * LOG2E


def dot_nn(a, b):
    return lax.dot_general(a, b, (((1,), (0,)), ((), ())), preferred_element_type=F32)


def thirds(value):
    first = value.astype(BF16)
    rest = value - first.astype(F32)
    second = rest.astype(BF16)
    third = (rest - second.astype(F32)).astype(BF16)
    return first, second, third


def split3(value):
    return jnp.concatenate(thirds(value), axis=0)


def product(dot, pieces, high, low):
    rows = pieces.shape[0] // 3
    big = dot(pieces, high)
    small = dot(pieces[: 2 * rows], low)
    return (big[:rows] + (big[rows : 2 * rows] + small[:rows])) + (big[2 * rows :] + small[rows:])


def ring(distance, count):
    return min(distance, count - distance)


FAR = sorted(
    [(j, k) for j in range(NY) for k in range(NZ) if j + k > 0],
    key=lambda jk: (-ring(jk[0], NY) - ring(jk[1], NZ), jk),
)
COL_ORDER = (4, 5, 3, 2, 6, 7, 1)
Z_ORDER = (4, 3, 5, 2, 6, 1, 7)
LINES = (NC - 1) + len(FAR)


def kernel(
    rhs_hbm,
    coords_hbm,
    nugget_hbm,
    ids_ref,
    basis_ref,
    sol_ref,
    res_ref,
    stage,
    bh,
    bl,
    bth,
    btl,
    th,
    tl,
    cext,
    nugget_ref,
    chalo,
    fs,
    dirn,
    wvec,
    qvec,
    zvec,
    halo,
    prs,
    p01,
    recv_top,
    recv_low,
    recv01,
    twin_send,
    recv_twin,
    recv_z,
    ysend,
    recv_y,
    tfull,
    top_res,
    top_dir,
    wide,
    scs,
    scr,
    gate,
    bsem,
    isem,
    csem,
    hsem,
    s_top,
    s_low,
    s01,
    s_twin,
    s_z,
    s_y,
    sg1,
    sg2,
    ssc,
    cs_send,
    hs_send,
    s_top_send,
    s_low_send,
    s01_send,
    s_twin_send,
    s_z_send,
    s_y_send,
    sg1_send,
    sg2_send,
    ssc_send,
):
    row = lax.axis_index("row")
    col = lax.axis_index("col")
    yy = row // NZ
    zz = row % NZ
    hh = col // 4
    gg = col % 4
    dev = row * NC + col
    right_dev = (dev + 1) % NDEV
    left_dev = (dev + NDEV - 1) % NDEV
    right = (right_dev // NC, right_dev % NC)
    left = (left_dev // NC, left_dev % NC)
    cpeers = [(row, (col + k) % NC) for k in range(1, NC)]
    zpeers = [(yy * NZ + (zz + k) % NZ, col) for k in range(1, NZ)]
    ypeers = [(((yy + k) % NY) * NZ + zz, col) for k in range(1, NY)]
    fpeers = [(((yy + j) % NY) * NZ + (zz + k) % NZ, col) for j, k in FAR]
    quad = [(row, (col // 4) * 4 + (col % 4 + k) % 4) for k in range(1, 4)]
    core = (row, col + 1 - 2 * (col % 2))
    twin = (yy * NZ + zz + 1 - 2 * (zz % 2), col)
    my_rows = pl.ds(pl.multiple_of(gg * 8, 8), 8)

    loads = [
        pltpu.make_async_copy(rhs_hbm, qvec, isem.at[0]),
        pltpu.make_async_copy(coords_hbm, cext.at[:, LEAF : LEAF + WIDTH], isem.at[1]),
        pltpu.make_async_copy(nugget_hbm, nugget_ref, isem.at[2]),
    ]
    loads[0].start()
    for level in (8, 9, 6, 7, 4, 5, 2, 3, 0, 1):
        pltpu.make_async_copy(basis_ref.at[level], stage.at[level], bsem.at[level]).start()
    loads[1].start()
    loads[2].start()
    barrier = pltpu.get_barrier_semaphore()
    greeted = zpeers + cpeers + ypeers + [left, right]
    for peer in greeted:
        pl.semaphore_signal(barrier, inc=1, device_id=peer, device_id_type=MESH)

    def send(src, dst, send_sem, recv_sem, peer):
        pltpu.make_async_remote_copy(
            src_ref=src, dst_ref=dst, send_sem=send_sem, recv_sem=recv_sem, device_id=peer, device_id_type=MESH
        ).start()

    def await_bytes(ref, sem):
        pltpu.make_async_copy(ref, ref, sem).wait()

    lane = lax.broadcasted_iota(jnp.int32, (NRHS, 128), 1)
    sub = lax.broadcasted_iota(jnp.int32, (NRHS, 128), 0)
    hit = (lane % NRHS) == sub

    def as_row(columns):
        spread = jnp.zeros((NRHS, 128), F32)
        for index, column in enumerate(columns):
            spread = jnp.where(hit & (lane // NRHS == index), column, spread)
        return jnp.sum(spread, axis=0, keepdims=True)

    def as_columns(line):
        wide = jnp.where(hit, jnp.broadcast_to(line, (NRHS, 128)), 0.0)
        return [
            jnp.sum(jnp.where(lane // NRHS == index, wide, 0.0), axis=1, keepdims=True)
            for index in range(4)
        ]

    def dots_row():
        r, d, q = res_ref[...], dirn[...], qvec[...]
        return as_row(
            [
                jnp.sum(r * r, axis=1, keepdims=True),
                jnp.sum(d * q, axis=1, keepdims=True),
                jnp.sum(r * q, axis=1, keepdims=True),
                jnp.sum(q * q, axis=1, keepdims=True),
            ]
        )

    def scalar_send(a, phase, peers, base):
        order = {NC - 1: COL_ORDER if phase == 0 else Z_ORDER}.get(len(peers), range(1, len(peers) + 1))
        for k in order:
            send(scs.at[a, phase], scr.at[a, base + k - 1], ssc_send.at[a, phase], ssc.at[a, phase], peers[k - 1])

    def scalar_gather(a, phase, count, base):
        await_bytes(scr.at[a, pl.ds(base, count)], ssc.at[a, phase])
        total = scs[a, phase]
        for k in range(count):
            total = total + scr[a, base + k]
        return total

    def load_levels(levels):
        for level in levels:
            pltpu.make_async_copy(basis_ref.at[level], stage.at[level], bsem.at[level]).wait()
            rows = slice(level * RANK, (level + 1) * RANK)
            value = stage[level]
            high = value.astype(BF16)
            bh[rows, :] = high
            bl[rows, :] = (value - high.astype(F32)).astype(BF16)
            value = jnp.transpose(stage[level])
            high = value.astype(BF16)
            bth[:, rows] = high
            btl[:, rows] = (value - high.astype(F32)).astype(BF16)

    def own(start, width):
        return fs[:, LEAF + start : LEAF + start + width]

    def skeleton_pair(a, level):
        rows = slice(level * RANK, (level + 2) * RANK)
        both = product(dot_nn, own(0, WIDTH), bth[:, rows], btl[:, rows])
        for side in range(2):
            part = both[:, side * RANK : (side + 1) * RANK]
            if level == 2:
                p01[a, side] = part
            else:
                prs[a, side, (level - 4) // 2] = part

    def scaled_pieces(levels, total):
        scaled = jnp.concatenate([t * (1.0 / (LEAF * 2 ** (level + 1))) for level, t in zip(levels, total)], axis=1)
        return split3(scaled), slice(levels[0] * RANK, (levels[-1] + 1) * RANK)

    def spread(levels, total):
        pieces, rows = scaled_pieces(levels, total)
        for start in range(0, WIDTH, 512):
            span = slice(start, start + 512)
            zvec[:, span] += product(dot_nn, pieces, bh[rows, span], bl[rows, span])

    def local_levels():
        rows = slice(0, 2 * RANK)
        half = WIDTH // 2
        spans = [slice(0, half), slice(half, WIDTH)]
        parts = [product(dot_nn, own(span.start, half), bth[span, rows], btl[span, rows]) for span in spans]
        whole = (parts[0][:, RANK:] + parts[1][:, RANK:]) * (1.0 / WIDTH)
        for span, part in zip(spans, parts):
            pieces = split3(jnp.concatenate([part[:, :RANK] * (1.0 / half), whole], axis=1))
            zvec[:, span] += product(dot_nn, pieces, bh[rows, span], bl[rows, span])

    def mask_value(leaf, offset):
        target = dev * LEAVES + leaf + offset - 1
        found = (ids_ref[leaf, 0] == target) | (ids_ref[leaf, 1] == target) | (ids_ref[leaf, 2] == target)
        return jnp.where(found & (target >= 0), 1.0, 0.0).astype(F32)

    def near(leaf):
        span = slice(leaf * LEAF, (leaf + 1) * LEAF)
        window = fs[:, leaf * LEAF : (leaf + 3) * LEAF]
        zvec[:, span] += product(dot_nn, window, th[leaf], tl[leaf])

    def take_halo(a, side):
        await_bytes(halo.at[a, side], hsem.at[a, side])
        start = side * (LEAF + WIDTH)
        fs[:, start : start + LEAF] = split3(halo[a, side])

    def center(leaf):
        first = cext[:, LEAF * (leaf + 1) : LEAF * (leaf + 1) + 128]
        return jnp.floor(first[:, 0:1]) + 0.5

    def features(points):
        parts = [part.astype(F32) for part in thirds(points)]
        norm = jnp.sum(points * points, axis=0, keepdims=True)
        return parts, [part.astype(F32) for part in thirds(norm)]

    def build(leaf):
        middle = center(leaf)
        (one, two, three), norms = features((cext[:, LEAF * (leaf + 1) : LEAF * (leaf + 2)] - middle) * SCALE)
        ones = jnp.ones((3, LEAF), F32)
        blank = jnp.zeros((8, LEAF), F32)
        here = jnp.concatenate([one, two, one, two, three, one], axis=0) * -2.0
        here = jnp.concatenate([here, ones] + norms + [blank], axis=0).astype(BF16)

        def block(offset, carry):
            start = pl.multiple_of((leaf + offset) * LEAF, LEAF)
            (one, two, three), norms = features((cext[:, pl.ds(start, LEAF)] - middle) * SCALE)
            there = jnp.concatenate([one, one, two, two, one, three] + norms + [ones, blank], axis=0)
            square = dot_nn(jnp.transpose(there).astype(BF16), here)
            square = jnp.maximum(square, 1e-30)
            dist = square * lax.rsqrt(square)
            weight = mask_value(leaf, offset) * (1.0 / 48.0)
            value = (weight + (weight * (1.0 / LOG2E)) * dist) * jnp.exp2(-dist)
            high = value.astype(BF16)
            rows = pl.ds(pl.multiple_of(offset * LEAF, LEAF), LEAF)
            th[leaf, rows, :] = high
            tl[leaf, rows, :] = (value - high.astype(F32)).astype(BF16)
            return carry

        lax.fori_loop(0, 3, block, 0)

    def eighth(k):
        other = (col + k) % NC
        return other // 4, pl.ds(pl.multiple_of((other % 4) * 8, 8), 8)

    def apply(a, first):
        if first:
            load_levels([8, 9, 6, 7])
            skeleton_pair(a, 8)
            skeleton_pair(a, 6)
            pl.semaphore_wait(barrier, len(greeted))
        else:
            skeleton_pair(a, 8)
            skeleton_pair(a, 6)
        for k in COL_ORDER:
            half, rows = eighth(k)
            part = prs.at[a, half, pl.ds(1, 2), rows, :]
            send(part, recv_top.at[a, k - 1], s_top_send.at[a], s_top.at[a], cpeers[k - 1])
        if first:
            for peer in ypeers:
                pl.semaphore_signal(gate, inc=1, device_id=peer, device_id_type=MESH)
            load_levels([4, 5])
        else:
            scs[a, 0] = dots_row()
            scalar_send(a, 0, cpeers, 0)
        skeleton_pair(a, 4)
        for k in COL_ORDER:
            half, rows = eighth(k)
            send(prs.at[a, half, 0, rows, :], recv_low.at[a, k - 1], s_low_send.at[a], s_low.at[a], cpeers[k - 1])
        send(qvec.at[:, 0:LEAF], halo.at[a, 1], hs_send.at[a, 1], hsem.at[a, 1], left)
        send(qvec.at[:, WIDTH - LEAF : WIDTH], halo.at[a, 0], hs_send.at[a, 0], hsem.at[a, 0], right)
        if first:
            loads[1].wait()
            loads[2].wait()
            send(cext.at[:, LEAF : 2 * LEAF], chalo.at[1], cs_send.at[1], csem.at[1], left)
            send(cext.at[:, WIDTH : WIDTH + LEAF], chalo.at[0], cs_send.at[0], csem.at[0], right)
            load_levels([2, 3])
        skeleton_pair(a, 2)
        send(p01.at[a, 0], recv01.at[a, 0], s01_send.at[a], s01.at[a], core)
        for k in range(3):
            send(p01.at[a, 1], recv01.at[a, k + 1], s01_send.at[a], s01.at[a], quad[k])

        def edge(side):
            leaf = side * (LEAVES - 1)
            if first:
                await_bytes(chalo.at[side], csem.at[side])
                start = side * (LEAF + WIDTH)
                cext[:, start : start + LEAF] = chalo[side]
                build(leaf)
            take_halo(a, side)
            near(leaf)

        zvec[...] = nugget_ref[...] * qvec[...]
        if first:
            build(1)
        near(1)

        await_bytes(recv_top.at[a], s_top.at[a])
        for t in range(2):
            total = prs[a, hh, t + 1, my_rows, :]
            for k in range(NC - 1):
                total = total + recv_top[a, k, t]
            ysend[a, t] = total
        if first:
            pl.semaphore_wait(gate, len(ypeers))
        for n, (j, k) in enumerate(FAR):
            if j == 0:
                send(ysend.at[a], recv_z.at[a, k - 1], s_z_send.at[a], s_z.at[a], fpeers[n])
            else:
                slot = (j - 1) * NZ + k
                send(ysend.at[a, 1], recv_y.at[a, slot], s_y_send.at[a], s_y.at[a], fpeers[n])
        if not first:
            scs[a, 1] = scalar_gather(a, 0, NC - 1, 0)
            scalar_send(a, 1, zpeers, NC - 1)
        await_bytes(recv_low.at[a], s_low.at[a])
        total = prs[a, hh, 0, my_rows, :]
        for k in range(NC - 1):
            total = total + recv_low[a, k]
        twin_send[a] = total
        send(twin_send.at[a], recv_twin.at[a], s_twin_send.at[a], s_twin.at[a], twin)

        if first:
            build(2)
        near(2)
        edge(0)
        if not first:
            edge(1)
        await_bytes(recv_twin.at[a], s_twin.at[a])
        tfull[a, hh, 0, my_rows, :] = twin_send[a] + hh.astype(F32) * recv_twin[a]
        mine = tfull.at[a, hh, 0, my_rows, :]
        for k in COL_ORDER:
            send(mine, mine, sg1_send.at[a], sg1.at[a], cpeers[k - 1])
        if first:
            load_levels([0, 1])
        local_levels()
        if not first:
            scs[a, 2] = scalar_gather(a, 1, NZ - 1, NC - 1)
            scalar_send(a, 2, ypeers, NC + NZ - 2)

        await_bytes(recv_z.at[a], s_z.at[a])
        await_bytes(recv_y.at[a], s_y.at[a])
        one = ysend[a, 0]
        two = ysend[a, 1]
        for k in range(1, NZ):
            source = (zz + NZ - k) % NZ
            quarter = jnp.where((hh == 1) | (source // 4 == zz // 4), 1.0, 0.0).astype(F32)
            one = one + quarter * recv_z[a, k - 1, 0]
            two = two + recv_z[a, k - 1, 1]
        for j in range(1, NY):
            source = (yy + NY - j) % NY
            half = jnp.where((hh == 1) | (source // 2 == yy // 2), 1.0, 0.0).astype(F32)
            ring_sum = recv_y[a, (j - 1) * NZ]
            for k in range(1, NZ):
                ring_sum = ring_sum + recv_y[a, (j - 1) * NZ + k]
            two = two + half * ring_sum
        tfull[a, hh, 1, my_rows, :] = one
        tfull[a, hh, 2, my_rows, :] = two
        mine = tfull.at[a, hh, pl.ds(1, 2), my_rows, :]
        for k in COL_ORDER:
            send(mine, mine, sg2_send.at[a], sg2.at[a], cpeers[k - 1])

        if first:
            edge(1)
        await_bytes(recv01.at[a], s01.at[a])
        pair = p01[a, 0] + recv01[a, 0]
        four = (p01[a, 1] + recv01[a, 1]) + (recv01[a, 2] + recv01[a, 3])
        await_bytes(recv_low.at[a], sg1.at[a])
        spread(list(range(2, 6)), [pair, four, tfull[a, 0, 0], tfull[a, 1, 0]])
        await_bytes(halo.at[a, 0], hs_send.at[a, 0])
        await_bytes(halo.at[a, 1], hs_send.at[a, 1])

    def top_levels(a, finish):
        await_bytes(recv_top.at[a], sg2.at[a])
        levels = [tfull[a, 0, 1], tfull[a, 1, 1], tfull[a, 0, 2], tfull[a, 1, 2]]
        pieces, rows = scaled_pieces(list(range(6, 10)), levels)
        for start in range(0, WIDTH, 512):
            span = slice(start, start + 512)
            q = finish(span, product(dot_nn, pieces, bh[rows, span], bl[rows, span]))
            qvec[:, span] = q
            fs[:, LEAF + start : LEAF + start + 512] = split3(q)

    def steps(total):
        norm, curve, cross, square = as_columns(total)
        step = norm / curve
        fresh = jnp.maximum(norm - 2.0 * step * cross + step * step * square, 0.0)
        return step, fresh / norm

    loads[0].wait()
    start = qvec[...]
    fs[:, LEAF : LEAF + WIDTH] = split3(start)
    sol_ref[...] = jnp.zeros_like(sol_ref)
    res_ref[...] = start
    dirn[...] = start
    apply(0, True)

    def first_image(span, top):
        image = zvec[:, span] + top
        wvec[:, span] = image
        return image

    top_levels(0, first_image)

    def own_top(a, t):
        return tfull[a, hh, t + 1, my_rows, :]

    for t in range(2):
        top_res[t] = own_top(0, t)
        top_dir[t] = own_top(0, t)

    def iteration(a, carry):
        apply(a, False)
        step, ratio = steps(scalar_gather(a, 2, NY - 1, NC + NZ - 2))
        q = qvec[...]
        d = dirn[...]
        sol_ref[...] += step * d
        r = res_ref[...] - step * q
        res_ref[...] = r
        dirn[...] = r + ratio * d
        w = wvec[...] - step * zvec[...]
        wvec[...] = w
        qvec[...] = w + ratio * q

        wide[0] = jnp.broadcast_to(step, (NRHS, RANK))
        wide[1] = jnp.broadcast_to(ratio, (NRHS, RANK))
        step_rows = wide[0, my_rows, :]
        ratio_rows = wide[1, my_rows, :]
        for t in range(2):
            top_res[t] = top_res[t] - step_rows * own_top(a, t)
            top_dir[t] = top_res[t] + ratio_rows * top_dir[t]

        @pl.when(a == ITERS - 1)
        def _():
            share = jnp.where(hh == 1, 0.25, 1.0).astype(F32) * 2.0**-18
            part = top_dir[0] * own_top(a, 0) + (1.0 / 16.0) * (top_dir[1] * own_top(a, 1))
            part = jnp.sum(part * step_rows, axis=1, keepdims=True) * share
            wide[0] = jnp.zeros((NRHS, RANK), F32)
            wide[0, my_rows, :] = jnp.broadcast_to(part, (8, RANK))
            r = res_ref[...]
            curve = jnp.sum(dirn[...] * qvec[...], axis=1, keepdims=True) - wide[0][:, 0:1]
            scs[ITERS, 0] = as_row([jnp.sum(r * r, axis=1, keepdims=True), curve])
            scalar_send(ITERS, 0, cpeers, 0)

        def next_image(span, top):
            change = step * top
            wvec[:, span] -= change
            return qvec[:, span] - change

        top_levels(a, next_image)
        return carry

    lax.fori_loop(1, ITERS, iteration, 0)

    last = ITERS
    scs[last, 1] = scalar_gather(last, 0, NC - 1, 0)
    scalar_send(last, 1, fpeers, NC - 1)
    step, _ = steps(scalar_gather(last, 1, len(FAR), NC - 1))
    sol_ref[...] += step * dirn[...]
    res_ref[...] += -step * qvec[...]

    def drain(a, carry):
        await_bytes(recv_top.at[a], s_top_send.at[a])
        await_bytes(recv_low.at[a], s_low_send.at[a])
        await_bytes(recv01.at[a], s01_send.at[a])
        await_bytes(recv_twin.at[a], s_twin_send.at[a])
        await_bytes(recv_z.at[a], s_z_send.at[a])
        await_bytes(recv_y.at[a], s_y_send.at[a])
        await_bytes(recv_low.at[a], sg1_send.at[a])
        await_bytes(recv_top.at[a], sg2_send.at[a])
        return carry

    def drain_scalars(a, carry):
        for phase, (base, count) in enumerate(((0, NC - 1), (NC - 1, NZ - 1), (NC + NZ - 2, NY - 1))):
            await_bytes(scr.at[a, pl.ds(base, count)], ssc_send.at[a, phase])
        return carry

    lax.fori_loop(0, ITERS, drain, 0)
    lax.fori_loop(1, ITERS, drain_scalars, 0)
    await_bytes(scr.at[last, pl.ds(0, NC - 1)], ssc_send.at[last, 0])
    await_bytes(scr.at[last, pl.ds(NC - 1, len(FAR))], ssc_send.at[last, 1])
    for side in range(2):
        await_bytes(chalo.at[side], cs_send.at[side])


def per_device(rhs, coords, nugget, near_ids, basis):
    anywhere = pl.BlockSpec(memory_space=pl.ANY)
    vmem = pl.BlockSpec(memory_space=pltpu.VMEM)
    state = pltpu.VMEM((NRHS, WIDTH), F32)
    dma = pltpu.SemaphoreType.DMA
    n = ITERS
    scratch = [
        pltpu.VMEM((LEVELS, RANK, WIDTH), F32),
        pltpu.VMEM((LEVELS * RANK, WIDTH), BF16),
        pltpu.VMEM((LEVELS * RANK, WIDTH), BF16),
        pltpu.VMEM((WIDTH, LEVELS * RANK), BF16),
        pltpu.VMEM((WIDTH, LEVELS * RANK), BF16),
        pltpu.VMEM((LEAVES, 3 * LEAF, LEAF), BF16),
        pltpu.VMEM((LEAVES, 3 * LEAF, LEAF), BF16),
        pltpu.VMEM((3, WIDTH + 2 * LEAF), F32),
        pltpu.VMEM((1, WIDTH), F32),
        pltpu.VMEM((2, 3, LEAF), F32),
        pltpu.VMEM((3 * NRHS, WIDTH + 2 * LEAF), BF16),
        state,
        state,
        state,
        state,
        pltpu.VMEM((n, 2, NRHS, LEAF), F32),
        pltpu.VMEM((n, 2, 3, NRHS, RANK), F32),
        pltpu.VMEM((n, 2, NRHS, RANK), F32),
        pltpu.VMEM((n, NC - 1, 2, 8, RANK), F32),
        pltpu.VMEM((n, NC - 1, 8, RANK), F32),
        pltpu.VMEM((n, 4, NRHS, RANK), F32),
        pltpu.VMEM((n, 8, RANK), F32),
        pltpu.VMEM((n, 8, RANK), F32),
        pltpu.VMEM((n, NZ - 1, 2, 8, RANK), F32),
        pltpu.VMEM((n, 2, 8, RANK), F32),
        pltpu.VMEM((n, NZ * (NY - 1), 8, RANK), F32),
        pltpu.VMEM((n, 2, 3, NRHS, RANK), F32),
        pltpu.VMEM((2, 8, RANK), F32),
        pltpu.VMEM((2, 8, RANK), F32),
        pltpu.VMEM((2, NRHS, RANK), F32),
        pltpu.VMEM((n + 1, 3, 1, RANK), F32),
        pltpu.VMEM((n + 1, LINES, 1, RANK), F32),
        pltpu.SemaphoreType.REGULAR,
        dma((LEVELS,)),
        dma((3,)),
        dma((2,)),
        dma((n, 2)),
        dma((n,)),
        dma((n,)),
        dma((n,)),
        dma((n,)),
        dma((n,)),
        dma((n,)),
        dma((n,)),
        dma((n,)),
        dma((n + 1, 3)),
        dma((2,)),
        dma((n, 2)),
        dma((n,)),
        dma((n,)),
        dma((n,)),
        dma((n,)),
        dma((n,)),
        dma((n,)),
        dma((n,)),
        dma((n,)),
        dma((n + 1, 3)),
    ]
    parts = pl.pallas_call(
        kernel,
        out_shape=[pltpu.VMEM((NRHS, WIDTH), F32)] * 2,
        in_specs=[anywhere, anywhere, anywhere, pl.BlockSpec(memory_space=pltpu.SMEM), anywhere],
        out_specs=[vmem, vmem],
        scratch_shapes=scratch,
        compiler_params=pltpu.CompilerParams(
            collective_id=0, has_side_effects=True, vmem_limit_bytes=56 * 1024 * 1024
        ),
    )(rhs, coords, nugget.reshape(1, WIDTH), near_ids, basis)
    return tuple(parts)


def solution(mesh):
    placed = (
        P(None, ("row", "col")),
        P(None, ("row", "col")),
        P(("row", "col")),
        P(("row", "col"), None),
        P(None, None, ("row", "col")),
    )
    return jax.shard_map(
        per_device,
        mesh=mesh,
        in_specs=placed,
        out_specs=(P(None, ("row", "col")), P(None, ("row", "col"))),
        check_vma=False,
    )
```

```python
import functools

import jax
import jax.numpy as jnp
from jax import lax
from jax.experimental import pallas as pl
from jax.experimental.pallas import tpu as pltpu
from jax.sharding import PartitionSpec as P

LEAF = 512
ITERS = 4
RANK = 128
NRHS = 32
LEVELS = 10
LEAVES = 4
WIDTH = LEAF * LEAVES
NC, NZ, NY = 8, 8, 4
NDEV = NC * NZ * NY
MESH = pl.DeviceIdType.MESH
F32 = jnp.float32
BF16 = jnp.bfloat16

ROOT_THREE = 1.7320508075688772
LENGTH = 1.6 * LEAF ** (-1.0 / 3.0)
LOG2E = 1.4426950408889634
SCALE = ROOT_THREE / LENGTH * LOG2E


def dot_nn(a, b):
    return lax.dot_general(a, b, (((1,), (0,)), ((), ())), preferred_element_type=F32)


def thirds(value):
    first = value.astype(BF16)
    rest = value - first.astype(F32)
    second = rest.astype(BF16)
    third = (rest - second.astype(F32)).astype(BF16)
    return first, second, third


def split3(value):
    return jnp.concatenate(thirds(value), axis=0)


def product(dot, pieces, high, low):
    rows = pieces.shape[0] // 3
    big = dot(pieces, high)
    small = dot(pieces[: 2 * rows], low)
    return (big[:rows] + (big[rows : 2 * rows] + small[:rows])) + (big[2 * rows :] + small[rows:])


def ring(distance, count):
    return min(distance, count - distance)


FAR = sorted(
    [(j, k) for j in range(NY) for k in range(NZ) if j + k > 0],
    key=lambda jk: (-ring(jk[0], NY) - ring(jk[1], NZ), jk),
)
COL_ORDER = (4, 5, 3, 2, 6, 7, 1)
Z_ORDER = (4, 3, 5, 2, 6, 1, 7)
LINES = (NC - 1) + len(FAR)


def kernel(
    rhs_hbm,
    coords_hbm,
    nugget_hbm,
    ids_ref,
    basis_ref,
    sol_ref,
    res_ref,
    stage,
    bh,
    bl,
    bth,
    btl,
    th,
    tl,
    cext,
    nugget_ref,
    chalo,
    fs,
    dirn,
    wvec,
    qvec,
    zvec,
    halo,
    prs,
    p01,
    recv_top,
    recv_low,
    recv01,
    twin_send,
    recv_twin,
    recv_z,
    ysend,
    recv_y,
    tfull,
    top_res,
    top_dir,
    wide,
    scs,
    scr,
    gate,
    bsem,
    isem,
    csem,
    hsem,
    s_top,
    s_low,
    s01,
    s_twin,
    s_z,
    s_y,
    sg1,
    sg2,
    ssc,
    cs_send,
    hs_send,
    s_top_send,
    s_low_send,
    s01_send,
    s_twin_send,
    s_z_send,
    s_y_send,
    sg1_send,
    sg2_send,
    ssc_send,
):
    row = lax.axis_index("row")
    col = lax.axis_index("col")
    yy = row // NZ
    zz = row % NZ
    hh = col // 4
    gg = col % 4
    dev = row * NC + col
    right_dev = (dev + 1) % NDEV
    left_dev = (dev + NDEV - 1) % NDEV
    right = (right_dev // NC, right_dev % NC)
    left = (left_dev // NC, left_dev % NC)
    cpeers = [(row, (col + k) % NC) for k in range(1, NC)]
    zpeers = [(yy * NZ + (zz + k) % NZ, col) for k in range(1, NZ)]
    ypeers = [(((yy + k) % NY) * NZ + zz, col) for k in range(1, NY)]
    fpeers = [(((yy + j) % NY) * NZ + (zz + k) % NZ, col) for j, k in FAR]
    quad = [(row, (col // 4) * 4 + (col % 4 + k) % 4) for k in range(1, 4)]
    core = (row, col + 1 - 2 * (col % 2))
    twin = (yy * NZ + zz + 1 - 2 * (zz % 2), col)
    my_rows = pl.ds(pl.multiple_of(gg * 8, 8), 8)

    loads = [
        pltpu.make_async_copy(rhs_hbm, qvec, isem.at[0]),
        pltpu.make_async_copy(coords_hbm, cext.at[:, LEAF : LEAF + WIDTH], isem.at[1]),
        pltpu.make_async_copy(nugget_hbm, nugget_ref, isem.at[2]),
    ]
    def fetch(levels):
        for level in levels:
            pltpu.make_async_copy(basis_ref.at[level], stage.at[level], bsem.at[level]).start()

    loads[0].start()
    fetch((8, 9, 6, 7))
    barrier = pltpu.get_barrier_semaphore()
    greeted = [zpeers[k - 1] for k in Z_ORDER] + ypeers + [left, right] + [cpeers[k - 1] for k in COL_ORDER]
    for peer in greeted:
        pl.semaphore_signal(barrier, inc=1, device_id=peer, device_id_type=MESH)
    fetch((4, 5, 2, 3, 0, 1))
    loads[1].start()
    loads[2].start()

    def send(src, dst, send_sem, recv_sem, peer):
        pltpu.make_async_remote_copy(
            src_ref=src, dst_ref=dst, send_sem=send_sem, recv_sem=recv_sem, device_id=peer, device_id_type=MESH
        ).start()

    def await_bytes(ref, sem):
        pltpu.make_async_copy(ref, ref, sem).wait()

    lane = lax.broadcasted_iota(jnp.int32, (NRHS, 128), 1)
    sub = lax.broadcasted_iota(jnp.int32, (NRHS, 128), 0)
    hit = (lane % NRHS) == sub

    def as_row(columns):
        spread = jnp.zeros((NRHS, 128), F32)
        for index, column in enumerate(columns):
            spread = jnp.where(hit & (lane // NRHS == index), column, spread)
        return jnp.sum(spread, axis=0, keepdims=True)

    def as_columns(line):
        wide = jnp.where(hit, jnp.broadcast_to(line, (NRHS, 128)), 0.0)
        return [
            jnp.sum(jnp.where(lane // NRHS == index, wide, 0.0), axis=1, keepdims=True)
            for index in range(4)
        ]

    def dots_row():
        r, d, q = res_ref[...], dirn[...], qvec[...]
        return as_row(
            [
                jnp.sum(r * r, axis=1, keepdims=True),
                jnp.sum(d * q, axis=1, keepdims=True),
                jnp.sum(r * q, axis=1, keepdims=True),
                jnp.sum(q * q, axis=1, keepdims=True),
            ]
        )

    def scalar_send(a, phase, peers, base):
        order = {NC - 1: COL_ORDER if phase == 0 else Z_ORDER}.get(len(peers), range(1, len(peers) + 1))
        for k in order:
            send(scs.at[a, phase], scr.at[a, base + k - 1], ssc_send.at[a, phase], ssc.at[a, phase], peers[k - 1])

    def scalar_gather(a, phase, count, base):
        await_bytes(scr.at[a, pl.ds(base, count)], ssc.at[a, phase])
        total = scs[a, phase]
        for k in range(count):
            total = total + scr[a, base + k]
        return total

    def load_levels(levels):
        for level in levels:
            pltpu.make_async_copy(basis_ref.at[level], stage.at[level], bsem.at[level]).wait()
            rows = slice(level * RANK, (level + 1) * RANK)
            value = stage[level]
            high = value.astype(BF16)
            bh[rows, :] = high
            bl[rows, :] = (value - high.astype(F32)).astype(BF16)
            value = jnp.transpose(stage[level])
            high = value.astype(BF16)
            bth[:, rows] = high
            btl[:, rows] = (value - high.astype(F32)).astype(BF16)

    def own(start, width):
        return fs[:, LEAF + start : LEAF + start + width]

    def skeleton_pair(a, level):
        rows = slice(level * RANK, (level + 2) * RANK)
        both = product(dot_nn, own(0, WIDTH), bth[:, rows], btl[:, rows])
        for side in range(2):
            part = both[:, side * RANK : (side + 1) * RANK]
            if level == 2:
                p01[a, side] = part
            else:
                prs[a, side, (level - 4) // 2] = part

    def scaled_pieces(levels, total):
        scaled = jnp.concatenate([t * (1.0 / (LEAF * 2 ** (level + 1))) for level, t in zip(levels, total)], axis=1)
        return split3(scaled), slice(levels[0] * RANK, (levels[-1] + 1) * RANK)

    def spread(levels, total):
        pieces, rows = scaled_pieces(levels, total)
        for start in range(0, WIDTH, 512):
            span = slice(start, start + 512)
            zvec[:, span] += product(dot_nn, pieces, bh[rows, span], bl[rows, span])

    def local_levels():
        rows = slice(0, 2 * RANK)
        half = WIDTH // 2
        spans = [slice(0, half), slice(half, WIDTH)]
        parts = [product(dot_nn, own(span.start, half), bth[span, rows], btl[span, rows]) for span in spans]
        whole = (parts[0][:, RANK:] + parts[1][:, RANK:]) * (1.0 / WIDTH)
        for span, part in zip(spans, parts):
            pieces = split3(jnp.concatenate([part[:, :RANK] * (1.0 / half), whole], axis=1))
            zvec[:, span] += product(dot_nn, pieces, bh[rows, span], bl[rows, span])

    def mask_value(leaf, offset):
        target = dev * LEAVES + leaf + offset - 1
        found = (ids_ref[leaf, 0] == target) | (ids_ref[leaf, 1] == target) | (ids_ref[leaf, 2] == target)
        return jnp.where(found & (target >= 0), 1.0, 0.0).astype(F32)

    def near(leaf):
        span = slice(leaf * LEAF, (leaf + 1) * LEAF)
        window = fs[:, leaf * LEAF : (leaf + 3) * LEAF]
        zvec[:, span] += product(dot_nn, window, th[leaf], tl[leaf])

    def take_halo(a, side):
        await_bytes(halo.at[a, side], hsem.at[a, side])
        start = side * (LEAF + WIDTH)
        fs[:, start : start + LEAF] = split3(halo[a, side])

    def center(leaf):
        first = cext[:, LEAF * (leaf + 1) : LEAF * (leaf + 1) + 128]
        return jnp.floor(first[:, 0:1]) + 0.5

    def features(points):
        parts = [part.astype(F32) for part in thirds(points)]
        norm = jnp.sum(points * points, axis=0, keepdims=True)
        return parts, [part.astype(F32) for part in thirds(norm)]

    def build(leaf):
        middle = center(leaf)
        (one, two, three), norms = features((cext[:, LEAF * (leaf + 1) : LEAF * (leaf + 2)] - middle) * SCALE)
        ones = jnp.ones((3, LEAF), F32)
        blank = jnp.zeros((8, LEAF), F32)
        here = jnp.concatenate([one, two, one, two, three, one], axis=0) * -2.0
        here = jnp.concatenate([here, ones] + norms + [blank], axis=0).astype(BF16)

        def block(offset, carry):
            start = pl.multiple_of((leaf + offset) * LEAF, LEAF)
            (one, two, three), norms = features((cext[:, pl.ds(start, LEAF)] - middle) * SCALE)
            there = jnp.concatenate([one, one, two, two, one, three] + norms + [ones, blank], axis=0)
            square = dot_nn(jnp.transpose(there).astype(BF16), here)
            square = jnp.maximum(square, 1e-30)
            dist = square * lax.rsqrt(square)
            weight = mask_value(leaf, offset) * (1.0 / 48.0)
            value = (weight + (weight * (1.0 / LOG2E)) * dist) * jnp.exp2(-dist)
            high = value.astype(BF16)
            rows = pl.ds(pl.multiple_of(offset * LEAF, LEAF), LEAF)
            th[leaf, rows, :] = high
            tl[leaf, rows, :] = (value - high.astype(F32)).astype(BF16)
            return carry

        lax.fori_loop(0, 3, block, 0)

    def eighth(k):
        other = (col + k) % NC
        return other // 4, pl.ds(pl.multiple_of((other % 4) * 8, 8), 8)

    def apply(a, first):
        if first:
            load_levels([8, 9, 6, 7])
            skeleton_pair(a, 8)
            skeleton_pair(a, 6)
            pl.semaphore_wait(barrier, len(greeted))
        else:
            skeleton_pair(a, 8)
            skeleton_pair(a, 6)
        for k in COL_ORDER:
            half, rows = eighth(k)
            part = prs.at[a, half, pl.ds(1, 2), rows, :]
            send(part, recv_top.at[a, k - 1], s_top_send.at[a], s_top.at[a], cpeers[k - 1])
        if first:
            for peer in ypeers:
                pl.semaphore_signal(gate, inc=1, device_id=peer, device_id_type=MESH)
            load_levels([4, 5])
        else:
            scs[a, 0] = dots_row()
            scalar_send(a, 0, cpeers, 0)
        skeleton_pair(a, 4)
        for k in COL_ORDER:
            half, rows = eighth(k)
            send(prs.at[a, half, 0, rows, :], recv_low.at[a, k - 1], s_low_send.at[a], s_low.at[a], cpeers[k - 1])
        send(qvec.at[:, 0:LEAF], halo.at[a, 1], hs_send.at[a, 1], hsem.at[a, 1], left)
        send(qvec.at[:, WIDTH - LEAF : WIDTH], halo.at[a, 0], hs_send.at[a, 0], hsem.at[a, 0], right)
        if first:
            loads[1].wait()
            loads[2].wait()
            send(cext.at[:, LEAF : 2 * LEAF], chalo.at[1], cs_send.at[1], csem.at[1], left)
            send(cext.at[:, WIDTH : WIDTH + LEAF], chalo.at[0], cs_send.at[0], csem.at[0], right)
            load_levels([2, 3])
        skeleton_pair(a, 2)
        send(p01.at[a, 0], recv01.at[a, 0], s01_send.at[a], s01.at[a], core)
        for k in range(3):
            send(p01.at[a, 1], recv01.at[a, k + 1], s01_send.at[a], s01.at[a], quad[k])

        def edge(side):
            leaf = side * (LEAVES - 1)
            if first:
                await_bytes(chalo.at[side], csem.at[side])
                start = side * (LEAF + WIDTH)
                cext[:, start : start + LEAF] = chalo[side]
                build(leaf)
            take_halo(a, side)
            near(leaf)

        zvec[...] = nugget_ref[...] * qvec[...]
        if first:
            build(1)
        near(1)

        await_bytes(recv_top.at[a], s_top.at[a])
        for t in range(2):
            total = prs[a, hh, t + 1, my_rows, :]
            for k in range(NC - 1):
                total = total + recv_top[a, k, t]
            ysend[a, t] = total
        if first:
            pl.semaphore_wait(gate, len(ypeers))
        for n, (j, k) in enumerate(FAR):
            if j == 0:
                send(ysend.at[a], recv_z.at[a, k - 1], s_z_send.at[a], s_z.at[a], fpeers[n])
            else:
                slot = (j - 1) * NZ + k
                send(ysend.at[a, 1], recv_y.at[a, slot], s_y_send.at[a], s_y.at[a], fpeers[n])
        if not first:
            scs[a, 1] = scalar_gather(a, 0, NC - 1, 0)
            scalar_send(a, 1, zpeers, NC - 1)
        await_bytes(recv_low.at[a], s_low.at[a])
        total = prs[a, hh, 0, my_rows, :]
        for k in range(NC - 1):
            total = total + recv_low[a, k]
        twin_send[a] = total
        send(twin_send.at[a], recv_twin.at[a], s_twin_send.at[a], s_twin.at[a], twin)

        if first:
            build(2)
        near(2)
        edge(0)
        if not first:
            edge(1)
        await_bytes(recv_twin.at[a], s_twin.at[a])
        tfull[a, hh, 0, my_rows, :] = twin_send[a] + hh.astype(F32) * recv_twin[a]
        mine = tfull.at[a, hh, 0, my_rows, :]
        for k in COL_ORDER:
            send(mine, mine, sg1_send.at[a], sg1.at[a], cpeers[k - 1])
        if first:
            load_levels([0, 1])
        local_levels()
        if not first:
            scs[a, 2] = scalar_gather(a, 1, NZ - 1, NC - 1)
            scalar_send(a, 2, ypeers, NC + NZ - 2)

        await_bytes(recv_z.at[a], s_z.at[a])
        await_bytes(recv_y.at[a], s_y.at[a])
        one = ysend[a, 0]
        two = ysend[a, 1]
        for k in range(1, NZ):
            source = (zz + NZ - k) % NZ
            quarter = jnp.where((hh == 1) | (source // 4 == zz // 4), 1.0, 0.0).astype(F32)
            one = one + quarter * recv_z[a, k - 1, 0]
            two = two + recv_z[a, k - 1, 1]
        for j in range(1, NY):
            source = (yy + NY - j) % NY
            half = jnp.where((hh == 1) | (source // 2 == yy // 2), 1.0, 0.0).astype(F32)
            ring_sum = recv_y[a, (j - 1) * NZ]
            for k in range(1, NZ):
                ring_sum = ring_sum + recv_y[a, (j - 1) * NZ + k]
            two = two + half * ring_sum
        tfull[a, hh, 1, my_rows, :] = one
        tfull[a, hh, 2, my_rows, :] = two
        mine = tfull.at[a, hh, pl.ds(1, 2), my_rows, :]
        for k in COL_ORDER:
            send(mine, mine, sg2_send.at[a], sg2.at[a], cpeers[k - 1])

        if first:
            edge(1)
        await_bytes(recv01.at[a], s01.at[a])
        pair = p01[a, 0] + recv01[a, 0]
        four = (p01[a, 1] + recv01[a, 1]) + (recv01[a, 2] + recv01[a, 3])
        await_bytes(recv_low.at[a], sg1.at[a])
        spread(list(range(2, 6)), [pair, four, tfull[a, 0, 0], tfull[a, 1, 0]])
        await_bytes(halo.at[a, 0], hs_send.at[a, 0])
        await_bytes(halo.at[a, 1], hs_send.at[a, 1])

    def top_levels(a, finish):
        await_bytes(recv_top.at[a], sg2.at[a])
        levels = [tfull[a, 0, 1], tfull[a, 1, 1], tfull[a, 0, 2], tfull[a, 1, 2]]
        pieces, rows = scaled_pieces(list(range(6, 10)), levels)
        for start in range(0, WIDTH, 512):
            span = slice(start, start + 512)
            q = finish(span, product(dot_nn, pieces, bh[rows, span], bl[rows, span]))
            qvec[:, span] = q
            fs[:, LEAF + start : LEAF + start + 512] = split3(q)

    def steps(total):
        norm, curve, cross, square = as_columns(total)
        step = norm / curve
        fresh = jnp.maximum(norm - 2.0 * step * cross + step * step * square, 0.0)
        return step, fresh / norm

    loads[0].wait()
    start = qvec[...]
    fs[:, LEAF : LEAF + WIDTH] = split3(start)
    sol_ref[...] = jnp.zeros_like(sol_ref)
    res_ref[...] = start
    dirn[...] = start
    apply(0, True)

    def first_image(span, top):
        image = zvec[:, span] + top
        wvec[:, span] = image
        return image

    top_levels(0, first_image)

    def own_top(a, t):
        return tfull[a, hh, t + 1, my_rows, :]

    for t in range(2):
        top_res[t] = own_top(0, t)
        top_dir[t] = own_top(0, t)

    def iteration(a, carry):
        apply(a, False)
        step, ratio = steps(scalar_gather(a, 2, NY - 1, NC + NZ - 2))
        q = qvec[...]
        d = dirn[...]
        sol_ref[...] += step * d
        r = res_ref[...] - step * q
        res_ref[...] = r
        dirn[...] = r + ratio * d
        w = wvec[...] - step * zvec[...]
        wvec[...] = w
        qvec[...] = w + ratio * q

        wide[0] = jnp.broadcast_to(step, (NRHS, RANK))
        wide[1] = jnp.broadcast_to(ratio, (NRHS, RANK))
        step_rows = wide[0, my_rows, :]
        ratio_rows = wide[1, my_rows, :]
        for t in range(2):
            top_res[t] = top_res[t] - step_rows * own_top(a, t)
            top_dir[t] = top_res[t] + ratio_rows * top_dir[t]

        @pl.when(a == ITERS - 1)
        def _():
            share = jnp.where(hh == 1, 0.25, 1.0).astype(F32) * 2.0**-18
            part = top_dir[0] * own_top(a, 0) + (1.0 / 16.0) * (top_dir[1] * own_top(a, 1))
            part = jnp.sum(part * step_rows, axis=1, keepdims=True) * share
            wide[0] = jnp.zeros((NRHS, RANK), F32)
            wide[0, my_rows, :] = jnp.broadcast_to(part, (8, RANK))
            r = res_ref[...]
            curve = jnp.sum(dirn[...] * qvec[...], axis=1, keepdims=True) - wide[0][:, 0:1]
            scs[ITERS, 0] = as_row([jnp.sum(r * r, axis=1, keepdims=True), curve])
            scalar_send(ITERS, 0, cpeers, 0)

        def next_image(span, top):
            change = step * top
            wvec[:, span] -= change
            return qvec[:, span] - change

        top_levels(a, next_image)
        return carry

    lax.fori_loop(1, ITERS, iteration, 0)

    last = ITERS
    scs[last, 1] = scalar_gather(last, 0, NC - 1, 0)
    scalar_send(last, 1, fpeers, NC - 1)
    step, _ = steps(scalar_gather(last, 1, len(FAR), NC - 1))
    sol_ref[...] += step * dirn[...]
    res_ref[...] += -step * qvec[...]

    def drain(a, carry):
        await_bytes(recv_top.at[a], s_top_send.at[a])
        await_bytes(recv_low.at[a], s_low_send.at[a])
        await_bytes(recv01.at[a], s01_send.at[a])
        await_bytes(recv_twin.at[a], s_twin_send.at[a])
        await_bytes(recv_z.at[a], s_z_send.at[a])
        await_bytes(recv_y.at[a], s_y_send.at[a])
        await_bytes(recv_low.at[a], sg1_send.at[a])
        await_bytes(recv_top.at[a], sg2_send.at[a])
        return carry

    def drain_scalars(a, carry):
        for phase, (base, count) in enumerate(((0, NC - 1), (NC - 1, NZ - 1), (NC + NZ - 2, NY - 1))):
            await_bytes(scr.at[a, pl.ds(base, count)], ssc_send.at[a, phase])
        return carry

    lax.fori_loop(0, ITERS, drain, 0)
    lax.fori_loop(1, ITERS, drain_scalars, 0)
    await_bytes(scr.at[last, pl.ds(0, NC - 1)], ssc_send.at[last, 0])
    await_bytes(scr.at[last, pl.ds(NC - 1, len(FAR))], ssc_send.at[last, 1])
    for side in range(2):
        await_bytes(chalo.at[side], cs_send.at[side])


def per_device(rhs, coords, nugget, near_ids, basis):
    anywhere = pl.BlockSpec(memory_space=pl.ANY)
    vmem = pl.BlockSpec(memory_space=pltpu.VMEM)
    state = pltpu.VMEM((NRHS, WIDTH), F32)
    dma = pltpu.SemaphoreType.DMA
    n = ITERS
    scratch = [
        pltpu.VMEM((LEVELS, RANK, WIDTH), F32),
        pltpu.VMEM((LEVELS * RANK, WIDTH), BF16),
        pltpu.VMEM((LEVELS * RANK, WIDTH), BF16),
        pltpu.VMEM((WIDTH, LEVELS * RANK), BF16),
        pltpu.VMEM((WIDTH, LEVELS * RANK), BF16),
        pltpu.VMEM((LEAVES, 3 * LEAF, LEAF), BF16),
        pltpu.VMEM((LEAVES, 3 * LEAF, LEAF), BF16),
        pltpu.VMEM((3, WIDTH + 2 * LEAF), F32),
        pltpu.VMEM((1, WIDTH), F32),
        pltpu.VMEM((2, 3, LEAF), F32),
        pltpu.VMEM((3 * NRHS, WIDTH + 2 * LEAF), BF16),
        state,
        state,
        state,
        state,
        pltpu.VMEM((n, 2, NRHS, LEAF), F32),
        pltpu.VMEM((n, 2, 3, NRHS, RANK), F32),
        pltpu.VMEM((n, 2, NRHS, RANK), F32),
        pltpu.VMEM((n, NC - 1, 2, 8, RANK), F32),
        pltpu.VMEM((n, NC - 1, 8, RANK), F32),
        pltpu.VMEM((n, 4, NRHS, RANK), F32),
        pltpu.VMEM((n, 8, RANK), F32),
        pltpu.VMEM((n, 8, RANK), F32),
        pltpu.VMEM((n, NZ - 1, 2, 8, RANK), F32),
        pltpu.VMEM((n, 2, 8, RANK), F32),
        pltpu.VMEM((n, NZ * (NY - 1), 8, RANK), F32),
        pltpu.VMEM((n, 2, 3, NRHS, RANK), F32),
        pltpu.VMEM((2, 8, RANK), F32),
        pltpu.VMEM((2, 8, RANK), F32),
        pltpu.VMEM((2, NRHS, RANK), F32),
        pltpu.VMEM((n + 1, 3, 1, RANK), F32),
        pltpu.VMEM((n + 1, LINES, 1, RANK), F32),
        pltpu.SemaphoreType.REGULAR,
        dma((LEVELS,)),
        dma((3,)),
        dma((2,)),
        dma((n, 2)),
        dma((n,)),
        dma((n,)),
        dma((n,)),
        dma((n,)),
        dma((n,)),
        dma((n,)),
        dma((n,)),
        dma((n,)),
        dma((n + 1, 3)),
        dma((2,)),
        dma((n, 2)),
        dma((n,)),
        dma((n,)),
        dma((n,)),
        dma((n,)),
        dma((n,)),
        dma((n,)),
        dma((n,)),
        dma((n,)),
        dma((n + 1, 3)),
    ]
    parts = pl.pallas_call(
        kernel,
        out_shape=[pltpu.VMEM((NRHS, WIDTH), F32)] * 2,
        in_specs=[anywhere, anywhere, anywhere, pl.BlockSpec(memory_space=pltpu.SMEM), anywhere],
        out_specs=[vmem, vmem],
        scratch_shapes=scratch,
        compiler_params=pltpu.CompilerParams(
            collective_id=0, has_side_effects=True, vmem_limit_bytes=56 * 1024 * 1024
        ),
    )(rhs, coords, nugget.reshape(1, WIDTH), near_ids, basis)
    return tuple(parts)


def solution(mesh):
    placed = (
        P(None, ("row", "col")),
        P(None, ("row", "col")),
        P(("row", "col")),
        P(("row", "col"), None),
        P(None, None, ("row", "col")),
    )
    return jax.shard_map(
        per_device,
        mesh=mesh,
        in_specs=placed,
        out_specs=(P(None, ("row", "col")), P(None, ("row", "col"))),
        check_vma=False,
    )
```
